32 devices in a mesh: groups: 2 (over x), surf: 16 (over z, y, core).
Axes of the slice: x: 2, y: 2, z: 4, core: 2. Of those that a mesh axis runs over, the one named last changes fastest.
Arguments:
- sensitivity: bfloat16 [96, 131072], P(None, ('groups', 'surf')), parts along dimension 1, may hold values from -6 to 6
- owner: int32 [131072], P(('groups', 'surf')), parts along dimension 0, may hold values from 0 to 65535, as said below
- patch_count: int32 [32], P(('groups', 'surf')), parts along dimension 0, may hold values from 16 to 32, as said below
- neighbours: int32 [1024, 9], P(('groups', 'surf')), parts along dimension 0, may hold values from 0 to 511, as said below
- coupling: float32 [1024, 9], P(('groups', 'surf')), parts along dimension 0, may hold values from 0.25 to 2
Outputs:
- surface_grad: float32 [96, 131072], P(None, ('groups', 'surf')), parts along dimension 1
- smoothed: float32 [96, 131072], P(None, ('groups', 'surf')), parts along dimension 1
The draws below stay inside these ranges and needn't reach their ends.
There are 2 independent parts, one for each index of `groups`. The reference program is written for one: setup_inputs(seed, part) draws one part's arguments, and reference() takes and returns one part's arrays. A program takes and returns all parts, laid end to end along the dimension named above; each array names one. Nothing has to cross between parts.
Inputs may be any that keep to these rules, and one draw needn't show every extreme that they name: Each face's owner lies in the node range of its own partition or of a partition beside it, 4096 nodes a partition. `patch_count`: the first partition is full. `neighbours`: each neighbour differs from its patch by 1 to 4 in patch order.
All inputs are finite; a program needn't handle non-finite values.
Results may differ from the reference program's by a relative error of at most 0.0003.
Values may be sent and summed in bfloat16 or wider, within the bound.
A program may use at most 64 MiB of HBM per device.

```python
import math
import jax
import jax.numpy as jnp

COLS = 96
NODES = 128
NBR = 9
REACH = 4
SWEEPS = 4
PATCH_DEV = 32
FACE_DEV = 4096
PARTITIONS = 16
NPATCH = 512
FACES = 65536


def draw_owner(key, part):
    partitions = FACES // FACE_DEV
    faces_ids = jnp.arange(FACES, dtype=jnp.int32)
    home = faces_ids // FACE_DEV
    first_key, second_key = jax.random.split(key)
    delta = jax.random.randint(first_key, (FACES,), -1, 2, dtype=jnp.int32)
    target = home + delta
    target = jnp.where((target < 0) | (target >= partitions), home, target)
    span = PATCH_DEV * NODES
    return target * span + jax.random.randint(second_key, (FACES,), 0, span, dtype=jnp.int32)


def draw_patch_count(key, part):
    counts = jax.random.randint(key, (PARTITIONS,), (PATCH_DEV + 1) // 2, PATCH_DEV + 1, dtype=jnp.int32)
    return counts.at[0].set(PATCH_DEV)


def draw_neighbours(key, part):
    first_key, second_key = jax.random.split(jax.random.fold_in(key, 7))
    patch_ids = jnp.arange(NPATCH, dtype=jnp.int32)[:, None]
    offsets = jax.random.randint(first_key, (NPATCH, NBR), 1, REACH + 1, dtype=jnp.int32)
    offsets = offsets.at[:, 0].set(REACH)
    signs = 2 * jax.random.randint(second_key, (NPATCH, NBR), 0, 2, dtype=jnp.int32) - 1
    chosen = patch_ids + signs * offsets
    flipped = patch_ids - signs * offsets
    return jnp.where((chosen < 0) | (chosen >= NPATCH), flipped, chosen)


def block_levels(rng, dims, cuts, low, high):
    level = 1.0
    for axis_at, parts in cuts:
        draws = jax.random.uniform(jax.random.fold_in(jax.random.fold_in(rng, 6), axis_at), (parts,), jnp.float32, low / len(cuts), high / len(cuts))
        level = level * jnp.repeat(jnp.exp(draws), dims[axis_at] // parts).reshape((-1,) + (1,) * (len(dims) - 1 - axis_at))
    return level


def bell_draw(own_key, shape, spread, reach, cuts=(), kind=jnp.bfloat16):
    result = jax.random.normal(own_key, shape, jnp.float32) * spread
    if len(cuts) > 0:
        result = block_levels(own_key, shape, cuts, -0.22, 0.18) * result
    return jnp.clip(result, min=-reach, max=reach).astype(kind)


def setup_inputs(seed: int = 0, part: int = 0) -> dict:
    streams_of = jax.random.split(jax.random.key(seed), 6)
    part_splits = jax.random.split(jax.random.fold_in(streams_of[5], part), 6)
    sensitivity = bell_draw(part_splits[0], (COLS, FACES), 1.0, 6.0, ((1, 16),))
    owner = draw_owner(jax.random.fold_in(jax.random.fold_in(streams_of[5], part), 71), part)
    patch_count = draw_patch_count(jax.random.fold_in(jax.random.fold_in(streams_of[5], part), 71), part)
    neighbours = draw_neighbours(jax.random.fold_in(jax.random.fold_in(streams_of[5], part), 71), part)
    coupling = jnp.clip(jnp.exp(math.log(2.0) - 2.0794415 * jax.random.uniform(part_splits[4], (NPATCH, NBR), jnp.float32) ** block_levels(part_splits[4], (NPATCH, NBR), ((0, 16),), -0.2, 0.2)), 0.25, 2.0)
    return dict(sensitivity=sensitivity, owner=owner, patch_count=patch_count, neighbours=neighbours, coupling=coupling)


smoothing = 1.5


def reference(sensitivity, owner, patch_count, neighbours, coupling):
    total_nodes = NPATCH * NODES
    summed = jnp.zeros((COLS, total_nodes), jnp.float32).at[:, owner].add(sensitivity.astype(jnp.float32))
    patch_ids = jnp.arange(NPATCH, dtype=jnp.int32)
    alive = (patch_ids % PATCH_DEV < patch_count[patch_ids // PATCH_DEV]).astype(jnp.float32)
    surface = summed.reshape(COLS, NPATCH, NODES) * alive[None, :, None]
    diagonal = 1.0 + smoothing * (2.0 + jnp.sum(coupling, axis=1))
    field = surface
    for sweep in range(SWEEPS):
        links = jnp.roll(field, 1, axis=2) + jnp.roll(field, -1, axis=2)
        for entry in range(NBR):
            links = links + coupling[:, entry][None, :, None] * jnp.take(field, neighbours[:, entry], axis=1)
        field = alive[None, :, None] * (surface + smoothing * links) / diagonal[None, :, None]
    return surface.reshape(COLS, total_nodes), field.reshape(COLS, total_nodes)
```

```python
import functools

import jax
import jax.numpy as jnp
from jax import lax
from jax.experimental import pallas as pl
from jax.experimental.pallas import tpu as pltpu
from jax.sharding import PartitionSpec as P

NODES = 128
REACH = 4
SWEEPS = 4
LOW = 256
LANES = 128
PAIR = 2
BATCH = 8
smoothing = 1.5
OFFSETS = [d for d in range(-REACH, REACH + 1) if d != 0]
NOFF = len(OFFSETS)
MESH = pl.DeviceIdType.MESH


def kernel(
    chunk,
    sens,
    owner,
    count,
    neighbours_in,
    coupling_in,
    surface_stage,
    smooth_stage,
    neighbours,
    coupling,
    link_sem,
    values,
    owners,
    masked,
    low_hot,
    acc,
    fields,
    weights,
    table,
    halo_out,
    halo_in,
    out_sem,
    load_sem,
    oload_sem,
    send_sem,
    recv_sem,
    osend_sem,
    orecv_sem,
    hsend_sem,
    hrecv_sem,
):
    columns, faces = sens.shape
    patches = neighbours.shape[1]
    span = patches * NODES
    highs = span // LOW
    chunks = faces // chunk
    pieces = chunk // LANES
    orow = faces // LANES
    position = lax.axis_index("surf")
    peers = lax.axis_size("surf")
    has_below = position > 0
    has_above = position < peers - 1

    def local_load(k):
        return pltpu.make_async_copy(sens.at[:, pl.ds(k * chunk, chunk)], values.at[0, k], load_sem.at[k])

    def face_copy(side, k):
        target = position + 1 if side == 0 else position - 1
        return pltpu.make_async_remote_copy(
            src_ref=sens.at[:, pl.ds(k * chunk, chunk)],
            dst_ref=values.at[1 + side, k],
            send_sem=send_sem.at[side, k],
            recv_sem=recv_sem.at[side, k],
            device_id={"surf": target},
            device_id_type=MESH,
        )

    def owner_copy(side):
        target = position + 1 if side == 0 else position - 1
        return pltpu.make_async_remote_copy(
            src_ref=owner,
            dst_ref=owners.at[1 + side],
            send_sem=osend_sem.at[side],
            recv_sem=orecv_sem.at[side],
            device_id={"surf": target},
            device_id_type=MESH,
        )

    def halo_copy(side, sweep):
        target = position + 1 if side == 0 else position - 1
        if sweep == SWEEPS - 1:
            source = patches if side == 0 else REACH
            landing = 0 if side == 0 else patches + REACH
            src, dst = fields.at[sweep, pl.ds(source, REACH)], fields.at[sweep, pl.ds(landing, REACH)]
        else:
            src, dst = halo_out.at[side, sweep], halo_in.at[side, sweep]
        return pltpu.make_async_remote_copy(
            src_ref=src,
            dst_ref=dst,
            send_sem=hsend_sem.at[side, sweep],
            recv_sem=hrecv_sem.at[side, sweep],
            device_id={"surf": target},
            device_id_type=MESH,
        )

    own_owner = pltpu.make_async_copy(owner, owners.at[0], oload_sem)
    own_owner.start()
    link_copies = (
        pltpu.make_async_copy(neighbours_in, neighbours, link_sem.at[0]),
        pltpu.make_async_copy(coupling_in, coupling, link_sem.at[1]),
    )
    for link_copy in link_copies:
        link_copy.start()
    for k in range(chunks):
        local_load(k).start()

    barrier = pltpu.get_barrier_semaphore()

    @pl.when(has_below)
    def _():
        pl.semaphore_signal(barrier, inc=1, device_id={"surf": position - 1}, device_id_type=MESH)

    @pl.when(has_above)
    def _():
        pl.semaphore_signal(barrier, inc=1, device_id={"surf": position + 1}, device_id_type=MESH)

    both = jnp.logical_and(has_below, has_above)

    @pl.when(both)
    def _():
        pl.semaphore_wait(barrier, 2)

    @pl.when(jnp.logical_not(both))
    def _():
        pl.semaphore_wait(barrier, 1)

    @pl.when(has_above)
    def _():
        owner_copy(0).start()

    @pl.when(has_below)
    def _():
        owner_copy(1).start()

    for k in range(chunks):

        @pl.when(has_above)
        def _(k=k):
            face_copy(0, k).start()

        @pl.when(has_below)
        def _(k=k):
            face_copy(1, k).start()

    for link_copy in link_copies:
        link_copy.wait()
    slots = lax.broadcasted_iota(jnp.int32, neighbours.shape, 1)
    distance = neighbours[...] - (position * patches + slots)
    links = coupling[...]
    along = lax.broadcasted_iota(jnp.int32, (1, patches), 1)
    alive = jnp.where(along < count[0], 1.0, 0.0).astype(jnp.float32)
    share = alive / (1.0 + smoothing * (2.0 + jnp.sum(links, axis=0, keepdims=True)))
    lines = [
        smoothing * share * jnp.sum(jnp.where(distance == offset, links, 0.0), axis=0, keepdims=True)
        for offset in OFFSETS
    ]
    lines += [share, smoothing * share, alive]
    table[...] = jnp.zeros_like(table)
    for at, line in enumerate(lines):
        table[pl.ds(at, 1), pl.ds(0, patches)] = line
    turned = jnp.transpose(table[...])
    for at in range(len(lines)):
        line = jnp.broadcast_to(turned[0:patches, at : at + 1], (patches, LANES))
        weights[at] = jnp.broadcast_to(line[:, None, :], (patches, 8, LANES))

    zero_halo = jnp.zeros((REACH, columns, NODES), jnp.float32)

    @pl.when(jnp.logical_not(has_below))
    def _():
        for sweep in range(SWEEPS):
            fields[sweep, pl.ds(0, REACH)] = zero_halo

    @pl.when(jnp.logical_not(has_above))
    def _():
        for sweep in range(SWEEPS):
            fields[sweep, pl.ds(patches + REACH, REACH)] = zero_halo

    acc[...] = jnp.zeros_like(acc)
    first_node = position * span
    low_rows = lax.broadcasted_iota(jnp.int32, (LOW, LANES), 0)

    def add_chunk(slot, k):
        for j in range(pieces):
            local = owners[slot, pl.ds(k * pieces + j, 1), :] - first_node
            high = (local >> 8).astype(jnp.float32).astype(jnp.bfloat16)
            low = local & (LOW - 1)
            lanes = pl.ds(j * LANES, LANES)
            low_hot[:, lanes] = jnp.where(low_rows == low, 1.0, 0.0).astype(jnp.bfloat16)
            vals = values[slot, k, :, lanes]
            high_full = jnp.broadcast_to(high, vals.shape)
            for h in range(highs):
                masked[pl.ds(h * columns, columns), lanes] = jnp.where(
                    high_full == jnp.bfloat16(h), vals, jnp.bfloat16(0)
                )
        acc[...] += lax.dot_general(
            masked[...],
            low_hot[...],
            (((1,), (1,)), ((), ())),
            preferred_element_type=jnp.float32,
        )

    own_owner.wait()

    def step(s, carry):
        is_own = s < chunks
        t = jnp.maximum(s - chunks, 0)
        side = lax.rem(t, 2)
        k = jnp.where(is_own, s, t // 2)
        slot = jnp.where(is_own, 0, 1 + side)

        @pl.when(is_own)
        def _():
            local_load(k).wait()

        from_below = jnp.logical_and(jnp.logical_not(is_own), side == 0)
        from_above = jnp.logical_and(jnp.logical_not(is_own), side == 1)

        @pl.when(jnp.logical_and(from_below, has_below))
        def _():
            @pl.when(t == 0)
            def _():
                owner_copy(0).wait_recv()

            face_copy(0, k).wait_recv()

        @pl.when(jnp.logical_and(from_above, has_above))
        def _():
            @pl.when(t == 1)
            def _():
                owner_copy(1).wait_recv()

            face_copy(1, k).wait_recv()

        present = jnp.logical_or(
            is_own,
            jnp.logical_or(jnp.logical_and(side == 0, has_below), jnp.logical_and(side == 1, has_above)),
        )

        @pl.when(present)
        def _():
            add_chunk(slot, k)

        return carry

    lax.fori_loop(0, 3 * chunks, step, 0)

    def put_surface(h):
        for half in range(LOW // NODES):
            p = h * (LOW // NODES) + half
            patch = acc[pl.ds(h * columns, columns), pl.ds(half * NODES, NODES)]
            patch = patch * weights[NOFF + 2, p, 0:1, :]
            fields[0, REACH + p] = patch
            surface_stage[:, pl.ds(p * NODES, NODES)] = patch

    def send_halo(sweep):
        for side, there in ((0, has_above), (1, has_below)):

            @pl.when(there)
            def _(side=side):
                if sweep < SWEEPS - 1:
                    first = patches if side == 0 else REACH
                    halo_out[side, sweep] = fields[sweep, pl.ds(first, REACH)].astype(jnp.bfloat16)
                halo_copy(side, sweep).start()

    def wait_halo(sweep):
        for side, there in ((0, has_below), (1, has_above)):

            @pl.when(there)
            def _(side=side):
                halo_copy(side, sweep).wait_recv()
                if sweep < SWEEPS - 1:
                    first = 0 if side == 0 else patches + REACH
                    fields[sweep, pl.ds(first, REACH)] = halo_in[side, sweep].astype(jnp.float32)

    ends = REACH * NODES // LOW
    for h in list(range(ends)) + list(range(highs - ends, highs)):
        put_surface(h)
    send_halo(0)
    for h in range(ends, highs - ends):
        put_surface(h)


    def relax(sweep, first, count):
        for group in range(0, columns, 8 * PAIR):
            blocks = [pl.ds(group + 8 * k, 8) for k in range(PAIR)]
            window = [[fields[sweep, first + q, c, :] for q in range(2 * REACH)] for c in blocks]
            for at in range(count):
                p = first + at
                parts = [weights[line, p] for line in range(NOFF + 2)]
                for k, c in enumerate(blocks):
                    window[k].append(fields[sweep, p + 2 * REACH, c, :])
                    here = window[k][at + REACH]
                    terms = [parts[line] * window[k][at + REACH + offset] for line, offset in enumerate(OFFSETS)]
                    terms.append(parts[NOFF] * fields[0, p + REACH, c, :])
                    terms.append(parts[NOFF + 1] * (pltpu.roll(here, 1, 1) + pltpu.roll(here, NODES - 1, 1)))
                    while len(terms) > 1:
                        terms = [sum(terms[n : n + 2][1:], terms[n]) for n in range(0, len(terms), 2)]
                    if sweep == SWEEPS - 1:
                        smooth_stage[c, pl.ds(pl.multiple_of(p * NODES, NODES), NODES)] = terms[0]
                    else:
                        fields[sweep + 1, p + REACH, c, :] = terms[0]

    def relax_inner(sweep):
        def one(step, carry):
            relax(sweep, REACH + step * BATCH, BATCH)
            return carry

        lax.fori_loop(0, (patches - 2 * REACH) // BATCH, one, 0)

    for sweep in range(SWEEPS):
        last = sweep == SWEEPS - 1
        if last:
            relax_inner(sweep)
        wait_halo(sweep)
        relax(sweep, 0, REACH)
        relax(sweep, patches - REACH, REACH)
        if not last:
            send_halo(sweep + 1)
            relax_inner(sweep)

    for side, there in ((0, has_above), (1, has_below)):

        @pl.when(there)
        def _(side=side):
            owner_copy(side).wait_send()
            for k in range(chunks):
                face_copy(side, k).wait_send()
            for sweep in range(SWEEPS):
                halo_copy(side, sweep).wait_send()


def hand_over(surface, smooth, surface_out, smooth_out, out_sem):
    copies = [
        pltpu.make_async_copy(surface, surface_out, out_sem.at[0]),
        pltpu.make_async_copy(smooth, smooth_out, out_sem.at[1]),
    ]
    for copy in copies:
        copy.start()
    for copy in copies:
        copy.wait()


def body(sensitivity, owner, patch_count, neighbours, coupling):
    columns, faces = sensitivity.shape
    patches = neighbours.shape[0]
    span = patches * NODES
    chunk = min(512, faces)
    chunks = faces // chunk
    highs = span // LOW
    hbm = pl.BlockSpec(memory_space=pltpu.HBM)
    vmem = pl.BlockSpec(memory_space=pltpu.VMEM)
    links = neighbours.T.shape
    out = jax.ShapeDtypeStruct((columns, span), jnp.float32)
    dma = pltpu.SemaphoreType.DMA
    outputs = pl.pallas_call(
        functools.partial(kernel, chunk),
        out_shape=(pltpu.VMEM((columns, span), jnp.float32),) * 2,
        in_specs=[hbm, hbm, pl.BlockSpec(memory_space=pltpu.SMEM), hbm, hbm],
        out_specs=(vmem, vmem),
        scratch_shapes=[
            pltpu.VMEM(links, jnp.int32),
            pltpu.VMEM(links, jnp.float32),
            dma((2,)),
            pltpu.VMEM((3, chunks, columns, chunk), jnp.bfloat16),
            pltpu.VMEM((3, faces // LANES, LANES), jnp.int32),
            pltpu.VMEM((highs * columns, chunk), jnp.bfloat16),
            pltpu.VMEM((LOW, chunk), jnp.bfloat16),
            pltpu.VMEM((highs * columns, LOW), jnp.float32),
            pltpu.VMEM((SWEEPS, patches + 2 * REACH, columns, NODES), jnp.float32),
            pltpu.VMEM((NOFF + 3, patches, 8, LANES), jnp.float32),
            pltpu.VMEM((16, LANES), jnp.float32),
            pltpu.VMEM((2, SWEEPS - 1, REACH, columns, NODES), jnp.bfloat16),
            pltpu.VMEM((2, SWEEPS - 1, REACH, columns, NODES), jnp.bfloat16),
            dma((2,)),
            dma((chunks,)),
            dma,
            dma((2, chunks)),
            dma((2, chunks)),
            dma((2,)),
            dma((2,)),
            dma((2, SWEEPS)),
            dma((2, SWEEPS)),
        ],
        compiler_params=pltpu.CompilerParams(
            collective_id=0, has_side_effects=True, vmem_limit_bytes=60 * 1024 * 1024
        ),
    )(sensitivity, owner.reshape(faces // LANES, LANES), patch_count, neighbours.T, coupling.T)
    return pl.pallas_call(
        hand_over,
        out_shape=(out, out),
        in_specs=[vmem, vmem],
        out_specs=(hbm, hbm),
        scratch_shapes=[dma((2,))],
        compiler_params=pltpu.CompilerParams(vmem_limit_bytes=16 * 1024 * 1024),
    )(*outputs)


def solution(mesh):
    placed = (
        P(None, ("groups", "surf")),
        P(("groups", "surf")),
        P(("groups", "surf")),
        P(("groups", "surf"), None),
        P(("groups", "surf"), None),
    )
    return jax.shard_map(
        body,
        mesh=mesh,
        in_specs=placed,
        out_specs=(P(None, ("groups", "surf")), P(None, ("groups", "surf"))),
        check_vma=False,
    )
```

```python
import functools

import jax
import jax.numpy as jnp
from jax import lax
from jax.experimental import pallas as pl
from jax.experimental.pallas import tpu as pltpu
from jax.sharding import PartitionSpec as P

NODES = 128
REACH = 4
SWEEPS = 4
LOW = 256
LANES = 128
PAIR = 2
BATCH = 8
BLOCK = 512
SLOTS = 256
WIDE = 1024
VMEM_LIMIT = 60 * 1024 * 1024
smoothing = 1.5
OFFSETS = [d for d in range(-REACH, REACH + 1) if d != 0]
NOFF = len(OFFSETS)
MESH = pl.DeviceIdType.MESH


def prepare(count, neighbours, coupling, table, weights, fields):
    patches, columns = neighbours.shape[1], fields.shape[2]
    position = lax.axis_index("surf")
    has_below = position > 0
    has_above = position < lax.axis_size("surf") - 1
    slots = lax.broadcasted_iota(jnp.int32, neighbours.shape, 1)
    distance = neighbours[...] - (position * patches + slots)
    links = coupling[...]
    along = lax.broadcasted_iota(jnp.int32, (1, patches), 1)
    alive = jnp.where(along < count[0], 1.0, 0.0).astype(jnp.float32)
    share = alive / (1.0 + smoothing * (2.0 + jnp.sum(links, axis=0, keepdims=True)))
    lines = [
        smoothing * share * jnp.sum(jnp.where(distance == offset, links, 0.0), axis=0, keepdims=True)
        for offset in OFFSETS
    ]
    lines += [share, smoothing * share, alive]
    table[...] = jnp.zeros_like(table)
    for at, line in enumerate(lines):
        table[pl.ds(at, 1), pl.ds(0, patches)] = line
    turned = jnp.transpose(table[...])
    for at in range(len(lines)):
        line = jnp.broadcast_to(turned[0:patches, at : at + 1], (patches, LANES))
        weights[at] = jnp.broadcast_to(line[:, None, :], (patches, 8, LANES))

    zero_halo = jnp.zeros((REACH, columns, NODES), jnp.float32)

    @pl.when(jnp.logical_not(has_below))
    def _():
        for sweep in range(SWEEPS):
            fields[sweep, pl.ds(0, REACH)] = zero_halo

    @pl.when(jnp.logical_not(has_above))
    def _():
        for sweep in range(SWEEPS):
            fields[sweep, pl.ds(patches + REACH, REACH)] = zero_halo


def relaxation(acc, fields, weights, halo_out, halo_in, hsend_sem, hrecv_sem, surface_stage, smooth_stage, aside):
    columns = fields.shape[2]
    patches = fields.shape[1] - 2 * REACH
    highs = patches * NODES // LOW
    position = lax.axis_index("surf")
    has_below = position > 0
    has_above = position < lax.axis_size("surf") - 1

    def halo_copy(side, sweep):
        target = position + 1 if side == 0 else position - 1
        if sweep == SWEEPS - 1:
            source = patches if side == 0 else REACH
            landing = 0 if side == 0 else patches + REACH
            src, dst = fields.at[sweep, pl.ds(source, REACH)], fields.at[sweep, pl.ds(landing, REACH)]
        else:
            src, dst = halo_out.at[side, sweep], halo_in.at[side, sweep]
        return pltpu.make_async_remote_copy(
            src_ref=src,
            dst_ref=dst,
            send_sem=hsend_sem.at[side, sweep],
            recv_sem=hrecv_sem.at[side, sweep],
            device_id={"surf": target},
            device_id_type=MESH,
        )

    def put_surface(h):
        for half in range(LOW // NODES):
            p = h * (LOW // NODES) + half
            patch = acc[pl.ds(h * columns, columns), pl.ds(half * NODES, NODES)]
            patch = patch * weights[NOFF + 2, p, 0:1, :]
            fields[0, REACH + p] = patch
            surface_stage[:, pl.ds(p * NODES, NODES)] = patch

    def send_halo(sweep):
        for side, there in ((0, has_above), (1, has_below)):

            @pl.when(there)
            def _(side=side):
                if sweep < SWEEPS - 1:
                    first = patches if side == 0 else REACH
                    halo_out[side, sweep] = fields[sweep, pl.ds(first, REACH)].astype(jnp.bfloat16)
                halo_copy(side, sweep).start()

    def wait_halo(sweep):
        for side, there in ((0, has_below), (1, has_above)):

            @pl.when(there)
            def _(side=side):
                halo_copy(side, sweep).wait_recv()
                if sweep < SWEEPS - 1:
                    first = 0 if side == 0 else patches + REACH
                    fields[sweep, pl.ds(first, REACH)] = halo_in[side, sweep].astype(jnp.float32)

    ends = REACH * NODES // LOW
    for h in list(range(ends)) + list(range(highs - ends, highs)):
        put_surface(h)
    send_halo(0)
    for h in range(ends, highs - ends):
        put_surface(h)


    def relax(sweep, first, count):
        for group in range(0, columns, 8 * PAIR):
            blocks = [pl.ds(group + 8 * k, 8) for k in range(PAIR)]
            window = [[fields[sweep, first + q, c, :] for q in range(2 * REACH)] for c in blocks]
            for at in range(count):
                p = first + at
                parts = [weights[line, p] for line in range(NOFF + 2)]
                for k, c in enumerate(blocks):
                    window[k].append(fields[sweep, p + 2 * REACH, c, :])
                    here = window[k][at + REACH]
                    terms = [parts[line] * window[k][at + REACH + offset] for line, offset in enumerate(OFFSETS)]
                    terms.append(parts[NOFF] * fields[0, p + REACH, c, :])
                    terms.append(parts[NOFF + 1] * (pltpu.roll(here, 1, 1) + pltpu.roll(here, NODES - 1, 1)))
                    while len(terms) > 1:
                        terms = [sum(terms[n : n + 2][1:], terms[n]) for n in range(0, len(terms), 2)]
                    if sweep == SWEEPS - 1:
                        smooth_stage[c, pl.ds(pl.multiple_of(p * NODES, NODES), NODES)] = terms[0]
                    else:
                        fields[sweep + 1, p + REACH, c, :] = terms[0]

    def relax_inner(sweep):
        def one(step, carry):
            relax(sweep, REACH + step * BATCH, BATCH)
            return carry

        lax.fori_loop(0, (patches - 2 * REACH) // BATCH, one, 0)

    for sweep in range(SWEEPS):
        last = sweep == SWEEPS - 1
        if last:
            relax_inner(sweep)
        aside(sweep)
        wait_halo(sweep)
        relax(sweep, 0, REACH)
        relax(sweep, patches - REACH, REACH)
        if not last:
            send_halo(sweep + 1)
            relax_inner(sweep)

    for side, there in ((0, has_above), (1, has_below)):

        @pl.when(there)
        def _(side=side):
            for sweep in range(SWEEPS):
                halo_copy(side, sweep).wait_send()


def kernel(
    chunk,
    sens,
    owner,
    count,
    neighbours_in,
    coupling_in,
    surface_stage,
    smooth_stage,
    neighbours,
    coupling,
    link_sem,
    values,
    owners,
    masked,
    low_hot,
    acc,
    fields,
    weights,
    table,
    halo_out,
    halo_in,
    out_sem,
    load_sem,
    oload_sem,
    send_sem,
    recv_sem,
    osend_sem,
    orecv_sem,
    hsend_sem,
    hrecv_sem,
):
    columns, faces = sens.shape
    patches = neighbours.shape[1]
    span = patches * NODES
    highs = span // LOW
    chunks = faces // chunk
    pieces = chunk // LANES
    orow = faces // LANES
    position = lax.axis_index("surf")
    peers = lax.axis_size("surf")
    has_below = position > 0
    has_above = position < peers - 1

    def local_load(k):
        return pltpu.make_async_copy(sens.at[:, pl.ds(k * chunk, chunk)], values.at[0, k], load_sem.at[k])

    def face_copy(side, k):
        target = position + 1 if side == 0 else position - 1
        return pltpu.make_async_remote_copy(
            src_ref=sens.at[:, pl.ds(k * chunk, chunk)],
            dst_ref=values.at[1 + side, k],
            send_sem=send_sem.at[side, k],
            recv_sem=recv_sem.at[side, k],
            device_id={"surf": target},
            device_id_type=MESH,
        )

    def owner_copy(side):
        target = position + 1 if side == 0 else position - 1
        return pltpu.make_async_remote_copy(
            src_ref=owner,
            dst_ref=owners.at[1 + side],
            send_sem=osend_sem.at[side],
            recv_sem=orecv_sem.at[side],
            device_id={"surf": target},
            device_id_type=MESH,
        )

    own_owner = pltpu.make_async_copy(owner, owners.at[0], oload_sem)
    own_owner.start()
    link_copies = (
        pltpu.make_async_copy(neighbours_in, neighbours, link_sem.at[0]),
        pltpu.make_async_copy(coupling_in, coupling, link_sem.at[1]),
    )
    for link_copy in link_copies:
        link_copy.start()
    for k in range(chunks):
        local_load(k).start()

    barrier = pltpu.get_barrier_semaphore()

    @pl.when(has_below)
    def _():
        pl.semaphore_signal(barrier, inc=1, device_id={"surf": position - 1}, device_id_type=MESH)

    @pl.when(has_above)
    def _():
        pl.semaphore_signal(barrier, inc=1, device_id={"surf": position + 1}, device_id_type=MESH)

    both = jnp.logical_and(has_below, has_above)

    @pl.when(both)
    def _():
        pl.semaphore_wait(barrier, 2)

    @pl.when(jnp.logical_not(both))
    def _():
        pl.semaphore_wait(barrier, 1)

    @pl.when(has_above)
    def _():
        owner_copy(0).start()

    @pl.when(has_below)
    def _():
        owner_copy(1).start()

    for k in range(chunks):

        @pl.when(has_above)
        def _(k=k):
            face_copy(0, k).start()

        @pl.when(has_below)
        def _(k=k):
            face_copy(1, k).start()

    for link_copy in link_copies:
        link_copy.wait()
    prepare(count, neighbours, coupling, table, weights, fields)

    acc[...] = jnp.zeros_like(acc)
    first_node = position * span
    low_rows = lax.broadcasted_iota(jnp.int32, (LOW, LANES), 0)

    def add_chunk(slot, k):
        for j in range(pieces):
            local = owners[slot, pl.ds(k * pieces + j, 1), :] - first_node
            high = (local >> 8).astype(jnp.float32).astype(jnp.bfloat16)
            low = local & (LOW - 1)
            lanes = pl.ds(j * LANES, LANES)
            low_hot[:, lanes] = jnp.where(low_rows == low, 1.0, 0.0).astype(jnp.bfloat16)
            vals = values[slot, k, :, lanes]
            high_full = jnp.broadcast_to(high, vals.shape)
            for h in range(highs):
                masked[pl.ds(h * columns, columns), lanes] = jnp.where(
                    high_full == jnp.bfloat16(h), vals, jnp.bfloat16(0)
                )
        acc[...] += lax.dot_general(
            masked[...],
            low_hot[...],
            (((1,), (1,)), ((), ())),
            preferred_element_type=jnp.float32,
        )

    own_owner.wait()

    def step(s, carry):
        is_own = s < chunks
        t = jnp.maximum(s - chunks, 0)
        side = lax.rem(t, 2)
        k = jnp.where(is_own, s, t // 2)
        slot = jnp.where(is_own, 0, 1 + side)

        @pl.when(is_own)
        def _():
            local_load(k).wait()

        from_below = jnp.logical_and(jnp.logical_not(is_own), side == 0)
        from_above = jnp.logical_and(jnp.logical_not(is_own), side == 1)

        @pl.when(jnp.logical_and(from_below, has_below))
        def _():
            @pl.when(t == 0)
            def _():
                owner_copy(0).wait_recv()

            face_copy(0, k).wait_recv()

        @pl.when(jnp.logical_and(from_above, has_above))
        def _():
            @pl.when(t == 1)
            def _():
                owner_copy(1).wait_recv()

            face_copy(1, k).wait_recv()

        present = jnp.logical_or(
            is_own,
            jnp.logical_or(jnp.logical_and(side == 0, has_below), jnp.logical_and(side == 1, has_above)),
        )

        @pl.when(present)
        def _():
            add_chunk(slot, k)

        return carry

    lax.fori_loop(0, 3 * chunks, step, 0)

    relaxation(
        acc, fields, weights, halo_out, halo_in, hsend_sem, hrecv_sem, surface_stage, smooth_stage, lambda sweep: None
    )

    for side, there in ((0, has_above), (1, has_below)):

        @pl.when(there)
        def _(side=side):
            owner_copy(side).wait_send()
            for k in range(chunks):
                face_copy(side, k).wait_send()


def packed_kernel(
    sens,
    owner,
    count,
    neighbours_in,
    coupling_in,
    surface_stage,
    smooth_stage,
    full_out,
    neighbours,
    coupling,
    link_sem,
    values,
    owners,
    nodes,
    spots,
    values_out,
    nodes_out,
    sort_hot,
    masked,
    low_hot,
    acc,
    fields,
    weights,
    table,
    halo_out,
    halo_in,
    flags,
    flags_in,
    load_sem,
    oload_sem,
    send_sem,
    recv_sem,
    nsend_sem,
    nrecv_sem,
    hsend_sem,
    hrecv_sem,
    fsend_sem,
    frecv_sem,
):
    columns, faces = sens.shape
    patches = neighbours.shape[1]
    span = patches * NODES
    highs = span // LOW
    rows = faces // LANES
    owns = faces // WIDE
    blocks = faces // BLOCK
    pieces = WIDE // LANES
    fit = WIDE // SLOTS
    others = blocks // fit
    position = lax.axis_index("surf")
    peers = lax.axis_size("surf")
    rounds = peers.bit_length() - 1
    has_below = position > 0
    has_above = position < peers - 1
    first_node = position * span

    def partner(step):
        size = 2 ** step
        return position + size - 2 * size * (lax.div(position, size) % 2)

    def local_load(k):
        return pltpu.make_async_copy(sens.at[:, pl.ds(k * WIDE, WIDE)], values.at[k], load_sem.at[k])

    def value_copy(side, k, q):
        target = position + 1 if side == 0 else position - 1
        lanes = pl.ds(pl.multiple_of(q * SLOTS, SLOTS), SLOTS)
        return pltpu.make_async_remote_copy(
            src_ref=values_out.at[side, k, :, lanes],
            dst_ref=values.at[owns + 2 * k + side, :, lanes],
            send_sem=send_sem.at[side, k, q],
            recv_sem=recv_sem.at[side, k, q],
            device_id={"surf": target},
            device_id_type=MESH,
        )

    def node_copy(side, k):
        target = position + 1 if side == 0 else position - 1
        return pltpu.make_async_remote_copy(
            src_ref=nodes_out.at[side, k],
            dst_ref=nodes.at[owns + 2 * k + side],
            send_sem=nsend_sem.at[side, k],
            recv_sem=nrecv_sem.at[side, k],
            device_id={"surf": target},
            device_id_type=MESH,
        )

    def flag_copy(step):
        return pltpu.make_async_remote_copy(
            src_ref=flags.at[step],
            dst_ref=flags_in.at[step],
            send_sem=fsend_sem.at[step],
            recv_sem=frecv_sem.at[step],
            device_id={"surf": partner(step)},
            device_id_type=MESH,
        )

    own_owner = pltpu.make_async_copy(owner, owners, oload_sem)
    own_owner.start()
    for k in range(owns):
        local_load(k).start()
    link_copies = (
        pltpu.make_async_copy(neighbours_in, neighbours, link_sem.at[0]),
        pltpu.make_async_copy(coupling_in, coupling, link_sem.at[1]),
    )
    for link_copy in link_copies:
        link_copy.start()

    barrier = pltpu.get_barrier_semaphore()

    @pl.when(has_below)
    def _():
        pl.semaphore_signal(barrier, inc=1, device_id={"surf": position - 1}, device_id_type=MESH)

    @pl.when(has_above)
    def _():
        pl.semaphore_signal(barrier, inc=1, device_id={"surf": position + 1}, device_id_type=MESH)

    for step in range(rounds):
        pl.semaphore_signal(barrier, inc=1, device_id={"surf": partner(step)}, device_id_type=MESH)

    own_owner.wait()
    local = owners[...] - first_node
    for k in range(owns):
        nodes[k] = local[k * pieces : (k + 1) * pieces]
    leaves = jnp.concatenate([local - (span - 1), -local], axis=0) > 0
    marks = jnp.where(leaves, 1.0, 0.0).astype(jnp.bfloat16)
    down = lax.broadcasted_iota(jnp.int32, (LANES, LANES), 0)
    along = lax.broadcasted_iota(jnp.int32, (LANES, LANES), 1)
    earlier = jnp.where(down < along, 1.0, 0.0).astype(jnp.bfloat16)
    block_rows = BLOCK // LANES
    down = lax.broadcasted_iota(jnp.int32, (2 * rows, 2 * rows), 0)
    along = lax.broadcasted_iota(jnp.int32, (2 * rows, 2 * rows), 1)
    same = lax.div(down, block_rows) == lax.div(along, block_rows)
    above = jnp.where(same & (along < down), 1.0, 0.0).astype(jnp.bfloat16)
    sums = jnp.dot(marks, jnp.ones((LANES, LANES), jnp.bfloat16), preferred_element_type=jnp.float32)
    place = jnp.dot(marks, earlier, preferred_element_type=jnp.float32)
    place += jnp.dot(above, sums.astype(jnp.bfloat16), preferred_element_type=jnp.float32)
    spots[...] = jnp.where(leaves, place, 2.0 * SLOTS)
    over = jnp.where(leaves & (place > SLOTS - 0.5), 1.0, 0.0)
    flags[0] = functools.reduce(jnp.maximum, [over[8 * n : 8 * n + 8] for n in range(2 * rows // 8)])

    both = jnp.logical_and(has_below, has_above)

    @pl.when(both)
    def _():
        pl.semaphore_wait(barrier, 2 + rounds)

    @pl.when(jnp.logical_not(both))
    def _():
        pl.semaphore_wait(barrier, 1 + rounds)

    flag_copy(0).start()
    for k in range(owns):
        local_load(k).wait()

    slot_rows = lax.broadcasted_iota(jnp.int32, (SLOTS, LANES), 0).astype(jnp.float32).astype(jnp.bfloat16)
    code_rows = lax.broadcasted_iota(jnp.int32, (16, LANES), 0)
    in_wide = WIDE // BLOCK

    def pack(k, carry):
        for q in range(fit):
            at = k * fit + q
            codes = []
            for j in range(block_rows):
                lanes = pl.ds(j * LANES, LANES)
                row = at * block_rows + j
                node = owners[pl.ds(row, 1), :]
                high = jnp.broadcast_to((node >> 8) & (highs - 1), (16, LANES))
                low = jnp.broadcast_to(node & (LOW - 1), (16, LANES))
                code = jnp.where(code_rows == 0, high, jnp.where(code_rows == 1, low, 0))
                codes.append(code.astype(jnp.float32).astype(jnp.bfloat16))
                for side in range(2):
                    spot = spots[pl.ds(side * rows + row, 1), :].astype(jnp.bfloat16)
                    spot = jnp.broadcast_to(spot, (SLOTS, LANES))
                    sort_hot[q % 2, pl.ds(side * SLOTS, SLOTS), lanes] = jnp.where(
                        spot == slot_rows, jnp.bfloat16(1), jnp.bfloat16(0)
                    )
            own = values[k * (fit // in_wide) + q // in_wide, :, pl.ds((q % in_wide) * BLOCK, BLOCK)]
            left = jnp.concatenate([own, jnp.concatenate(codes, axis=1)], axis=0)
            moved = lax.dot_general(
                left, sort_hot[q % 2], (((1,), (1,)), ((), ())), preferred_element_type=jnp.float32
            )
            node = (moved[columns : columns + 1] * LOW + moved[columns + 1 : columns + 2]).astype(jnp.int32)
            for side, there in ((0, has_above), (1, has_below)):
                values_out[side, k, :, pl.ds(q * SLOTS, SLOTS)] = moved[
                    0:columns, side * SLOTS : (side + 1) * SLOTS
                ].astype(jnp.bfloat16)
                for j in range(SLOTS // LANES):
                    nodes_out[side, k, pl.ds(q * (SLOTS // LANES) + j, 1), :] = node[
                        :, side * SLOTS + j * LANES : side * SLOTS + (j + 1) * LANES
                    ]

                @pl.when(there)
                def _(side=side, q=q):
                    value_copy(side, k, q).start()

        for side, there in ((0, has_above), (1, has_below)):

            @pl.when(there)
            def _(side=side):
                node_copy(side, k).start()

        return carry

    lax.fori_loop(0, others, pack, 0)

    for link_copy in link_copies:
        link_copy.wait()
    prepare(count, neighbours, coupling, table, weights, fields)
    acc[...] = jnp.zeros_like(acc)

    def add_chunk(s):
        for j in range(pieces):
            node = nodes[s, pl.ds(j, 1), :]
            high = (node >> 8).astype(jnp.float32).astype(jnp.bfloat16)
            low = (node & (LOW - 1)).astype(jnp.float32).astype(jnp.bfloat16)
            lanes = pl.ds(j * LANES, LANES)
            low_hot[:, lanes] = jnp.where(
                slot_rows == jnp.broadcast_to(low, (LOW, LANES)), jnp.bfloat16(1), jnp.bfloat16(0)
            )
            vals = values[s, :, lanes]
            high_full = jnp.broadcast_to(high, vals.shape)
            for h in range(highs):
                masked[pl.ds(h * columns, columns), lanes] = jnp.where(
                    high_full == jnp.bfloat16(h), vals, jnp.bfloat16(0)
                )
        acc[...] += lax.dot_general(
            masked[...], low_hot[...], (((1,), (1,)), ((), ())), preferred_element_type=jnp.float32
        )

    def step(s, carry):
        t = jnp.maximum(s - owns, 0)
        side = lax.rem(t, 2)
        k = lax.div(t, 2)
        is_own = s < owns
        from_below = jnp.logical_and(jnp.logical_not(is_own), jnp.logical_and(side == 0, has_below))
        from_above = jnp.logical_and(jnp.logical_not(is_own), jnp.logical_and(side == 1, has_above))

        @pl.when(from_below)
        def _():
            node_copy(0, k).wait_recv()
            for q in range(fit):
                value_copy(0, k, q).wait_recv()

        @pl.when(from_above)
        def _():
            node_copy(1, k).wait_recv()
            for q in range(fit):
                value_copy(1, k, q).wait_recv()

        @pl.when(jnp.logical_or(is_own, jnp.logical_or(from_below, from_above)))
        def _():
            add_chunk(s)

        return carry

    lax.fori_loop(0, owns + 2 * others, step, 0)

    def pass_flags(step):
        flag_copy(step).wait_recv()
        flags[step + 1] = jnp.maximum(flags[step], flags_in[step])
        if step + 1 < rounds:
            flag_copy(step + 1).start()

    def aside(sweep):
        for step in range(rounds):
            if min(step, SWEEPS - 1) == sweep:
                pass_flags(step)

    relaxation(acc, fields, weights, halo_out, halo_in, hsend_sem, hrecv_sem, surface_stage, smooth_stage, aside)
    full_out[0] = jnp.max(flags[rounds]).astype(jnp.int32)

    for step in range(rounds):
        flag_copy(step).wait_send()
    for side, there in ((0, has_above), (1, has_below)):

        @pl.when(there)
        def _(side=side):
            for k in range(others):
                node_copy(side, k).wait_send()
                for q in range(fit):
                    value_copy(side, k, q).wait_send()


def hand_over(surface, smooth, surface_out, smooth_out, out_sem):
    copies = [
        pltpu.make_async_copy(surface, surface_out, out_sem.at[0]),
        pltpu.make_async_copy(smooth, smooth_out, out_sem.at[1]),
    ]
    for copy in copies:
        copy.start()
    for copy in copies:
        copy.wait()


def body(sensitivity, owner, patch_count, neighbours, coupling):
    columns, faces = sensitivity.shape
    patches = neighbours.shape[0]
    span = patches * NODES
    rows = faces // LANES
    chunk = min(512, faces)
    chunks = faces // chunk
    highs = span // LOW
    hbm = pl.BlockSpec(memory_space=pltpu.HBM)
    vmem = pl.BlockSpec(memory_space=pltpu.VMEM)
    smem = pl.BlockSpec(memory_space=pltpu.SMEM)
    links = neighbours.T.shape
    out = jax.ShapeDtypeStruct((columns, span), jnp.float32)
    kept = pltpu.VMEM((columns, span), jnp.float32)
    dma = pltpu.SemaphoreType.DMA
    operands = (sensitivity, owner.reshape(rows, LANES), patch_count, neighbours.T, coupling.T)
    peers = lax.axis_size("surf")
    link_scratch = [pltpu.VMEM(links, jnp.int32), pltpu.VMEM(links, jnp.float32), dma((2,))]
    field_scratch = [
        pltpu.VMEM((highs * columns, LOW), jnp.float32),
        pltpu.VMEM((SWEEPS, patches + 2 * REACH, columns, NODES), jnp.float32),
        pltpu.VMEM((NOFF + 3, patches, 8, LANES), jnp.float32),
        pltpu.VMEM((16, LANES), jnp.float32),
        pltpu.VMEM((2, SWEEPS - 1, REACH, columns, NODES), jnp.bfloat16),
        pltpu.VMEM((2, SWEEPS - 1, REACH, columns, NODES), jnp.bfloat16),
    ]

    def hand(outputs):
        return pl.pallas_call(
            hand_over,
            out_shape=(out, out),
            in_specs=[vmem, vmem],
            out_specs=(hbm, hbm),
            scratch_shapes=[dma((2,))],
            compiler_params=pltpu.CompilerParams(vmem_limit_bytes=16 * 1024 * 1024),
        )(*outputs)

    def whole():
        return pl.pallas_call(
            functools.partial(kernel, chunk),
            out_shape=(kept, kept),
            in_specs=[hbm, hbm, smem, hbm, hbm],
            out_specs=(vmem, vmem),
            scratch_shapes=[
                *link_scratch,
                pltpu.VMEM((3, chunks, columns, chunk), jnp.bfloat16),
                pltpu.VMEM((3, rows, LANES), jnp.int32),
                pltpu.VMEM((highs * columns, chunk), jnp.bfloat16),
                pltpu.VMEM((LOW, chunk), jnp.bfloat16),
                *field_scratch,
                dma((2,)),
                dma((chunks,)),
                dma,
                dma((2, chunks)),
                dma((2, chunks)),
                dma((2,)),
                dma((2,)),
                dma((2, SWEEPS)),
                dma((2, SWEEPS)),
            ],
            compiler_params=pltpu.CompilerParams(
                collective_id=0, has_side_effects=True, vmem_limit_bytes=VMEM_LIMIT
            ),
        )(*operands)

    if faces % WIDE or highs & (highs - 1) or peers & (peers - 1):
        return hand(whole())

    owns, blocks, fit, rounds = faces // WIDE, faces // BLOCK, WIDE // SLOTS, peers.bit_length() - 1
    others = blocks // fit
    surface, smooth, full = pl.pallas_call(
        packed_kernel,
        out_shape=(kept, kept, jax.ShapeDtypeStruct((1,), jnp.int32)),
        in_specs=[hbm, hbm, smem, hbm, hbm],
        out_specs=(vmem, vmem, smem),
        scratch_shapes=[
            *link_scratch,
            pltpu.VMEM((owns + 2 * others, columns, WIDE), jnp.bfloat16),
            pltpu.VMEM((rows, LANES), jnp.int32),
            pltpu.VMEM((owns + 2 * others, WIDE // LANES, LANES), jnp.int32),
            pltpu.VMEM((2 * rows, LANES), jnp.float32),
            pltpu.VMEM((2, others, columns, WIDE), jnp.bfloat16),
            pltpu.VMEM((2, others, WIDE // LANES, LANES), jnp.int32),
            pltpu.VMEM((2, 2 * SLOTS, BLOCK), jnp.bfloat16),
            pltpu.VMEM((highs * columns, WIDE), jnp.bfloat16),
            pltpu.VMEM((LOW, WIDE), jnp.bfloat16),
            *field_scratch,
            pltpu.VMEM((rounds + 1, 8, LANES), jnp.float32),
            pltpu.VMEM((rounds, 8, LANES), jnp.float32),
            dma((owns,)),
            dma,
            dma((2, others, fit)),
            dma((2, others, fit)),
            dma((2, others)),
            dma((2, others)),
            dma((2, SWEEPS)),
            dma((2, SWEEPS)),
            dma((rounds,)),
            dma((rounds,)),
        ],
        compiler_params=pltpu.CompilerParams(collective_id=1, has_side_effects=True, vmem_limit_bytes=VMEM_LIMIT),
    )(*operands)
    _, surface, smooth = lax.while_loop(
        lambda state: state[0] != 0, lambda state: (jnp.int32(0), *hand(whole())), (full[0], *hand((surface, smooth)))
    )
    return surface, smooth


def solution(mesh):
    placed = (
        P(None, ("groups", "surf")),
        P(("groups", "surf")),
        P(("groups", "surf")),
        P(("groups", "surf"), None),
        P(("groups", "surf"), None),
    )
    return jax.shard_map(
        body,
        mesh=mesh,
        in_specs=placed,
        out_specs=(P(None, ("groups", "surf")), P(None, ("groups", "surf"))),
        check_vma=False,
    )
```

```python
import functools

import jax
import jax.numpy as jnp
from jax import lax
from jax.experimental import pallas as pl
from jax.experimental.pallas import tpu as pltpu
from jax.sharding import PartitionSpec as P

NODES = 128
REACH = 4
SWEEPS = 4
LOW = 256
LANES = 128
PAIR = 2
BATCH = 8
BLOCK = 512
SLOTS = 256
WIDE = 1024
GROUP = 48
LEVELS = 32766.0
TINY = 1e-33
VMEM_LIMIT = 60 * 1024 * 1024
smoothing = 1.5
OFFSETS = [d for d in range(-REACH, REACH + 1) if d != 0]
NOFF = len(OFFSETS)
MESH = pl.DeviceIdType.MESH


def prepare(count, neighbours, coupling, table, weights, fields):
    patches, columns = neighbours.shape[1], fields.shape[2]
    position = lax.axis_index("surf")
    has_below = position > 0
    has_above = position < lax.axis_size("surf") - 1
    slots = lax.broadcasted_iota(jnp.int32, neighbours.shape, 1)
    distance = neighbours[...] - (position * patches + slots)
    links = coupling[...]
    along = lax.broadcasted_iota(jnp.int32, (1, patches), 1)
    alive = jnp.where(along < count[0], 1.0, 0.0).astype(jnp.float32)
    share = alive / (1.0 + smoothing * (2.0 + jnp.sum(links, axis=0, keepdims=True)))
    lines = [
        smoothing * share * jnp.sum(jnp.where(distance == offset, links, 0.0), axis=0, keepdims=True)
        for offset in OFFSETS
    ]
    lines += [share, smoothing * share, alive]
    table[...] = jnp.zeros_like(table)
    for at, line in enumerate(lines):
        table[pl.ds(at, 1), pl.ds(0, patches)] = line
    turned = jnp.transpose(table[...])
    for at in range(len(lines)):
        line = jnp.broadcast_to(turned[0:patches, at : at + 1], (patches, LANES))
        weights[at] = jnp.broadcast_to(line[:, None, :], (patches, 8, LANES))

    zero_halo = jnp.zeros((REACH, columns, NODES), jnp.float32)

    @pl.when(jnp.logical_not(has_below))
    def _():
        for sweep in range(SWEEPS):
            fields[sweep, pl.ds(0, REACH)] = zero_halo

    @pl.when(jnp.logical_not(has_above))
    def _():
        for sweep in range(SWEEPS):
            fields[sweep, pl.ds(patches + REACH, REACH)] = zero_halo


def relaxation(acc, fields, weights, halos, surface_stage, smooth_stage, aside):
    halo_out, halo_in, scale_out, scale_in, hsend_sem, hrecv_sem, ssend_sem, srecv_sem = halos
    columns = fields.shape[2]
    patches = fields.shape[1] - 2 * REACH
    highs = patches * NODES // LOW
    groups = columns // GROUP
    position = lax.axis_index("surf")
    has_below = position > 0
    has_above = position < lax.axis_size("surf") - 1

    def halo_copies(side, sweep, g):
        target = position + 1 if side == 0 else position - 1
        return [
            pltpu.make_async_remote_copy(
                src_ref=src.at[side, sweep, g],
                dst_ref=dst.at[side, sweep, g],
                send_sem=send.at[side, sweep, g],
                recv_sem=recv.at[side, sweep, g],
                device_id={"surf": target},
                device_id_type=MESH,
            )
            for src, dst, send, recv in (
                (scale_out, scale_in, ssend_sem, srecv_sem),
                (halo_out, halo_in, hsend_sem, hrecv_sem),
            )
        ]

    def put_surface(h, g):
        rows = pl.ds(g * GROUP, GROUP)
        for half in range(LOW // NODES):
            p = h * (LOW // NODES) + half
            patch = acc[pl.ds(h * columns + g * GROUP, GROUP), pl.ds(half * NODES, NODES)]
            patch = patch * weights[NOFF + 2, p, 0:1, :]
            fields[0, REACH + p, rows] = patch
            surface_stage[rows, pl.ds(p * NODES, NODES)] = patch

    def spread(tile):
        return jnp.concatenate([tile] * (GROUP // 8), axis=0)[None]

    def send_halo(sweep, g):
        for side, there in ((0, has_above), (1, has_below)):

            @pl.when(there)
            def _(side=side):
                first = patches if side == 0 else REACH
                patch = fields[sweep, pl.ds(first, REACH), pl.ds(g * GROUP, GROUP)]
                size = jnp.abs(patch)
                peak = functools.reduce(
                    jnp.maximum, [size[q, 8 * n : 8 * n + 8] for q in range(REACH) for n in range(GROUP // 8)]
                )
                peak = jnp.maximum(peak, TINY)
                scale_out[side, sweep, g] = peak * (1.0 / LEVELS)
                code = jnp.floor(patch * spread(LEVELS / peak) + 0.5)
                halo_out[side, sweep, g] = code.astype(jnp.int32).astype(jnp.int16)
                for copy in halo_copies(side, sweep, g):
                    copy.start()

    def wait_halo(sweep, g):
        for side, there in ((0, has_below), (1, has_above)):

            @pl.when(there)
            def _(side=side):
                for copy in halo_copies(side, sweep, g):
                    copy.wait_recv()
                first = 0 if side == 0 else patches + REACH
                code = halo_in[side, sweep, g].astype(jnp.int32).astype(jnp.float32)
                fields[sweep, pl.ds(first, REACH), pl.ds(g * GROUP, GROUP)] = code * spread(scale_in[side, sweep, g])

    def relax(sweep, g, first, count):
        for low in range(g * GROUP, (g + 1) * GROUP, 8 * PAIR):
            blocks = [pl.ds(low + 8 * k, 8) for k in range(PAIR)]
            window = [[fields[sweep, first + q, c, :] for q in range(2 * REACH)] for c in blocks]
            for at in range(count):
                p = first + at
                parts = [weights[line, p] for line in range(NOFF + 2)]
                for k, c in enumerate(blocks):
                    window[k].append(fields[sweep, p + 2 * REACH, c, :])
                    here = window[k][at + REACH]
                    terms = [parts[line] * window[k][at + REACH + offset] for line, offset in enumerate(OFFSETS)]
                    terms.append(parts[NOFF] * fields[0, p + REACH, c, :])
                    terms.append(parts[NOFF + 1] * (pltpu.roll(here, 1, 1) + pltpu.roll(here, NODES - 1, 1)))
                    while len(terms) > 1:
                        terms = [sum(terms[n : n + 2][1:], terms[n]) for n in range(0, len(terms), 2)]
                    if sweep == SWEEPS - 1:
                        smooth_stage[c, pl.ds(pl.multiple_of(p * NODES, NODES), NODES)] = terms[0]
                    else:
                        fields[sweep + 1, p + REACH, c, :] = terms[0]

    def relax_inner(sweep, g):
        def one(step, carry):
            relax(sweep, g, REACH + step * BATCH, BATCH)
            return carry

        lax.fori_loop(0, (patches - 2 * REACH) // BATCH, one, 0)

    ends = REACH * NODES // LOW
    for g in range(groups):
        for h in list(range(ends)) + list(range(highs - ends, highs)):
            put_surface(h, g)
        send_halo(0, g)
    for h in range(ends, highs - ends):
        for g in range(groups):
            put_surface(h, g)

    for sweep in range(SWEEPS):
        last = sweep == SWEEPS - 1
        if last:
            for g in range(groups):
                relax_inner(sweep, g)
        aside(sweep)
        for g in range(groups):
            wait_halo(sweep, g)
            relax(sweep, g, 0, REACH)
            relax(sweep, g, patches - REACH, REACH)
            if not last:
                send_halo(sweep + 1, g)
                relax_inner(sweep, g)

    for side, there in ((0, has_above), (1, has_below)):

        @pl.when(there)
        def _(side=side):
            for sweep in range(SWEEPS):
                for g in range(groups):
                    for copy in halo_copies(side, sweep, g):
                        copy.wait_send()


def kernel(
    chunk,
    sens,
    owner,
    count,
    neighbours_in,
    coupling_in,
    surface_stage,
    smooth_stage,
    neighbours,
    coupling,
    link_sem,
    values,
    owners,
    masked,
    low_hot,
    acc,
    fields,
    weights,
    table,
    halo_out,
    halo_in,
    scale_out,
    scale_in,
    out_sem,
    load_sem,
    oload_sem,
    send_sem,
    recv_sem,
    osend_sem,
    orecv_sem,
    hsend_sem,
    hrecv_sem,
    ssend_sem,
    srecv_sem,
):
    columns, faces = sens.shape
    patches = neighbours.shape[1]
    span = patches * NODES
    highs = span // LOW
    chunks = faces // chunk
    pieces = chunk // LANES
    orow = faces // LANES
    position = lax.axis_index("surf")
    peers = lax.axis_size("surf")
    has_below = position > 0
    has_above = position < peers - 1

    def local_load(k):
        return pltpu.make_async_copy(sens.at[:, pl.ds(k * chunk, chunk)], values.at[0, k], load_sem.at[k])

    def face_copy(side, k):
        target = position + 1 if side == 0 else position - 1
        return pltpu.make_async_remote_copy(
            src_ref=sens.at[:, pl.ds(k * chunk, chunk)],
            dst_ref=values.at[1 + side, k],
            send_sem=send_sem.at[side, k],
            recv_sem=recv_sem.at[side, k],
            device_id={"surf": target},
            device_id_type=MESH,
        )

    def owner_copy(side):
        target = position + 1 if side == 0 else position - 1
        return pltpu.make_async_remote_copy(
            src_ref=owner,
            dst_ref=owners.at[1 + side],
            send_sem=osend_sem.at[side],
            recv_sem=orecv_sem.at[side],
            device_id={"surf": target},
            device_id_type=MESH,
        )

    own_owner = pltpu.make_async_copy(owner, owners.at[0], oload_sem)
    own_owner.start()
    link_copies = (
        pltpu.make_async_copy(neighbours_in, neighbours, link_sem.at[0]),
        pltpu.make_async_copy(coupling_in, coupling, link_sem.at[1]),
    )
    for link_copy in link_copies:
        link_copy.start()
    for k in range(chunks):
        local_load(k).start()

    barrier = pltpu.get_barrier_semaphore()

    @pl.when(has_below)
    def _():
        pl.semaphore_signal(barrier, inc=1, device_id={"surf": position - 1}, device_id_type=MESH)

    @pl.when(has_above)
    def _():
        pl.semaphore_signal(barrier, inc=1, device_id={"surf": position + 1}, device_id_type=MESH)

    both = jnp.logical_and(has_below, has_above)

    @pl.when(both)
    def _():
        pl.semaphore_wait(barrier, 2)

    @pl.when(jnp.logical_not(both))
    def _():
        pl.semaphore_wait(barrier, 1)

    @pl.when(has_above)
    def _():
        owner_copy(0).start()

    @pl.when(has_below)
    def _():
        owner_copy(1).start()

    for k in range(chunks):

        @pl.when(has_above)
        def _(k=k):
            face_copy(0, k).start()

        @pl.when(has_below)
        def _(k=k):
            face_copy(1, k).start()

    for link_copy in link_copies:
        link_copy.wait()
    prepare(count, neighbours, coupling, table, weights, fields)

    acc[...] = jnp.zeros_like(acc)
    first_node = position * span
    low_rows = lax.broadcasted_iota(jnp.int32, (LOW, LANES), 0)

    def add_chunk(slot, k):
        for j in range(pieces):
            local = owners[slot, pl.ds(k * pieces + j, 1), :] - first_node
            high = (local >> 8).astype(jnp.float32).astype(jnp.bfloat16)
            low = local & (LOW - 1)
            lanes = pl.ds(j * LANES, LANES)
            low_hot[:, lanes] = jnp.where(low_rows == low, 1.0, 0.0).astype(jnp.bfloat16)
            vals = values[slot, k, :, lanes]
            high_full = jnp.broadcast_to(high, vals.shape)
            for h in range(highs):
                masked[pl.ds(h * columns, columns), lanes] = jnp.where(
                    high_full == jnp.bfloat16(h), vals, jnp.bfloat16(0)
                )
        acc[...] += lax.dot_general(
            masked[...],
            low_hot[...],
            (((1,), (1,)), ((), ())),
            preferred_element_type=jnp.float32,
        )

    own_owner.wait()

    def step(s, carry):
        is_own = s < chunks
        t = jnp.maximum(s - chunks, 0)
        side = lax.rem(t, 2)
        k = jnp.where(is_own, s, t // 2)
        slot = jnp.where(is_own, 0, 1 + side)

        @pl.when(is_own)
        def _():
            local_load(k).wait()

        from_below = jnp.logical_and(jnp.logical_not(is_own), side == 0)
        from_above = jnp.logical_and(jnp.logical_not(is_own), side == 1)

        @pl.when(jnp.logical_and(from_below, has_below))
        def _():
            @pl.when(t == 0)
            def _():
                owner_copy(0).wait_recv()

            face_copy(0, k).wait_recv()

        @pl.when(jnp.logical_and(from_above, has_above))
        def _():
            @pl.when(t == 1)
            def _():
                owner_copy(1).wait_recv()

            face_copy(1, k).wait_recv()

        present = jnp.logical_or(
            is_own,
            jnp.logical_or(jnp.logical_and(side == 0, has_below), jnp.logical_and(side == 1, has_above)),
        )

        @pl.when(present)
        def _():
            add_chunk(slot, k)

        return carry

    lax.fori_loop(0, 3 * chunks, step, 0)

    halos = (halo_out, halo_in, scale_out, scale_in, hsend_sem, hrecv_sem, ssend_sem, srecv_sem)
    relaxation(acc, fields, weights, halos, surface_stage, smooth_stage, lambda sweep: None)

    for side, there in ((0, has_above), (1, has_below)):

        @pl.when(there)
        def _(side=side):
            owner_copy(side).wait_send()
            for k in range(chunks):
                face_copy(side, k).wait_send()


def packed_kernel(
    sens,
    owner,
    count,
    neighbours_in,
    coupling_in,
    surface_stage,
    smooth_stage,
    full_out,
    neighbours,
    coupling,
    link_sem,
    values,
    owners,
    nodes,
    spots,
    values_out,
    nodes_out,
    sort_hot,
    masked,
    low_hot,
    acc,
    fields,
    weights,
    table,
    halo_out,
    halo_in,
    scale_out,
    scale_in,
    flags,
    flags_in,
    load_sem,
    oload_sem,
    send_sem,
    recv_sem,
    nsend_sem,
    nrecv_sem,
    hsend_sem,
    hrecv_sem,
    ssend_sem,
    srecv_sem,
    fsend_sem,
    frecv_sem,
):
    columns, faces = sens.shape
    patches = neighbours.shape[1]
    span = patches * NODES
    highs = span // LOW
    rows = faces // LANES
    owns = faces // WIDE
    blocks = faces // BLOCK
    pieces = WIDE // LANES
    fit = WIDE // SLOTS
    others = blocks // fit
    position = lax.axis_index("surf")
    peers = lax.axis_size("surf")
    rounds = peers.bit_length() - 1
    has_below = position > 0
    has_above = position < peers - 1
    first_node = position * span

    def partner(step):
        size = 2 ** step
        return position + size - 2 * size * (lax.div(position, size) % 2)

    def local_load(k):
        return pltpu.make_async_copy(sens.at[:, pl.ds(k * WIDE, WIDE)], values.at[k], load_sem.at[k])

    def value_copy(side, k, q):
        target = position + 1 if side == 0 else position - 1
        lanes = pl.ds(pl.multiple_of(q * SLOTS, SLOTS), SLOTS)
        return pltpu.make_async_remote_copy(
            src_ref=values_out.at[side, k, :, lanes],
            dst_ref=values.at[owns + 2 * k + side, :, lanes],
            send_sem=send_sem.at[side, k, q],
            recv_sem=recv_sem.at[side, k, q],
            device_id={"surf": target},
            device_id_type=MESH,
        )

    def node_copy(side, k):
        target = position + 1 if side == 0 else position - 1
        return pltpu.make_async_remote_copy(
            src_ref=nodes_out.at[side, k],
            dst_ref=nodes.at[owns + 2 * k + side],
            send_sem=nsend_sem.at[side, k],
            recv_sem=nrecv_sem.at[side, k],
            device_id={"surf": target},
            device_id_type=MESH,
        )

    def flag_copy(step):
        return pltpu.make_async_remote_copy(
            src_ref=flags.at[step],
            dst_ref=flags_in.at[step],
            send_sem=fsend_sem.at[step],
            recv_sem=frecv_sem.at[step],
            device_id={"surf": partner(step)},
            device_id_type=MESH,
        )

    own_owner = pltpu.make_async_copy(owner, owners, oload_sem)
    own_owner.start()
    for k in range(owns):
        local_load(k).start()
    link_copies = (
        pltpu.make_async_copy(neighbours_in, neighbours, link_sem.at[0]),
        pltpu.make_async_copy(coupling_in, coupling, link_sem.at[1]),
    )
    for link_copy in link_copies:
        link_copy.start()

    barrier = pltpu.get_barrier_semaphore()

    @pl.when(has_below)
    def _():
        pl.semaphore_signal(barrier, inc=1, device_id={"surf": position - 1}, device_id_type=MESH)

    @pl.when(has_above)
    def _():
        pl.semaphore_signal(barrier, inc=1, device_id={"surf": position + 1}, device_id_type=MESH)

    for step in range(rounds):
        pl.semaphore_signal(barrier, inc=1, device_id={"surf": partner(step)}, device_id_type=MESH)

    own_owner.wait()
    local = owners[...] - first_node
    for k in range(owns):
        nodes[k] = local[k * pieces : (k + 1) * pieces]
    leaves = jnp.concatenate([local - (span - 1), -local], axis=0) > 0
    marks = jnp.where(leaves, 1.0, 0.0).astype(jnp.bfloat16)
    down = lax.broadcasted_iota(jnp.int32, (LANES, LANES), 0)
    along = lax.broadcasted_iota(jnp.int32, (LANES, LANES), 1)
    earlier = jnp.where(down < along, 1.0, 0.0).astype(jnp.bfloat16)
    block_rows = BLOCK // LANES
    down = lax.broadcasted_iota(jnp.int32, (2 * rows, 2 * rows), 0)
    along = lax.broadcasted_iota(jnp.int32, (2 * rows, 2 * rows), 1)
    same = lax.div(down, block_rows) == lax.div(along, block_rows)
    above = jnp.where(same & (along < down), 1.0, 0.0).astype(jnp.bfloat16)
    sums = jnp.dot(marks, jnp.ones((LANES, LANES), jnp.bfloat16), preferred_element_type=jnp.float32)
    place = jnp.dot(marks, earlier, preferred_element_type=jnp.float32)
    place += jnp.dot(above, sums.astype(jnp.bfloat16), preferred_element_type=jnp.float32)
    spots[...] = jnp.where(leaves, place, 2.0 * SLOTS)
    over = jnp.where(leaves & (place > SLOTS - 0.5), 1.0, 0.0)
    flags[0] = functools.reduce(jnp.maximum, [over[8 * n : 8 * n + 8] for n in range(2 * rows // 8)])

    both = jnp.logical_and(has_below, has_above)

    @pl.when(both)
    def _():
        pl.semaphore_wait(barrier, 2 + rounds)

    @pl.when(jnp.logical_not(both))
    def _():
        pl.semaphore_wait(barrier, 1 + rounds)

    flag_copy(0).start()
    for k in range(owns):
        local_load(k).wait()

    slot_rows = lax.broadcasted_iota(jnp.int32, (SLOTS, LANES), 0).astype(jnp.float32).astype(jnp.bfloat16)
    code_rows = lax.broadcasted_iota(jnp.int32, (16, LANES), 0)
    in_wide = WIDE // BLOCK

    def pack(k, carry):
        for q in range(fit):
            at = k * fit + q
            codes = []
            for j in range(block_rows):
                lanes = pl.ds(j * LANES, LANES)
                row = at * block_rows + j
                node = owners[pl.ds(row, 1), :]
                high = jnp.broadcast_to((node >> 8) & (highs - 1), (16, LANES))
                low = jnp.broadcast_to(node & (LOW - 1), (16, LANES))
                code = jnp.where(code_rows == 0, high, jnp.where(code_rows == 1, low, 0))
                codes.append(code.astype(jnp.float32).astype(jnp.bfloat16))
                for side in range(2):
                    spot = spots[pl.ds(side * rows + row, 1), :].astype(jnp.bfloat16)
                    spot = jnp.broadcast_to(spot, (SLOTS, LANES))
                    sort_hot[q % 2, pl.ds(side * SLOTS, SLOTS), lanes] = jnp.where(
                        spot == slot_rows, jnp.bfloat16(1), jnp.bfloat16(0)
                    )
            own = values[k * (fit // in_wide) + q // in_wide, :, pl.ds((q % in_wide) * BLOCK, BLOCK)]
            left = jnp.concatenate([own, jnp.concatenate(codes, axis=1)], axis=0)
            moved = lax.dot_general(
                left, sort_hot[q % 2], (((1,), (1,)), ((), ())), preferred_element_type=jnp.float32
            )
            node = (moved[columns : columns + 1] * LOW + moved[columns + 1 : columns + 2]).astype(jnp.int32)
            for side, there in ((0, has_above), (1, has_below)):
                values_out[side, k, :, pl.ds(q * SLOTS, SLOTS)] = moved[
                    0:columns, side * SLOTS : (side + 1) * SLOTS
                ].astype(jnp.bfloat16)
                for j in range(SLOTS // LANES):
                    nodes_out[side, k, pl.ds(q * (SLOTS // LANES) + j, 1), :] = node[
                        :, side * SLOTS + j * LANES : side * SLOTS + (j + 1) * LANES
                    ]

                @pl.when(there)
                def _(side=side, q=q):
                    value_copy(side, k, q).start()

        for side, there in ((0, has_above), (1, has_below)):

            @pl.when(there)
            def _(side=side):
                node_copy(side, k).start()

        return carry

    lax.fori_loop(0, others, pack, 0)

    for link_copy in link_copies:
        link_copy.wait()
    prepare(count, neighbours, coupling, table, weights, fields)
    acc[...] = jnp.zeros_like(acc)

    def add_chunk(s):
        for j in range(pieces):
            node = nodes[s, pl.ds(j, 1), :]
            high = (node >> 8).astype(jnp.float32).astype(jnp.bfloat16)
            low = (node & (LOW - 1)).astype(jnp.float32).astype(jnp.bfloat16)
            lanes = pl.ds(j * LANES, LANES)
            low_hot[:, lanes] = jnp.where(
                slot_rows == jnp.broadcast_to(low, (LOW, LANES)), jnp.bfloat16(1), jnp.bfloat16(0)
            )
            vals = values[s, :, lanes]
            high_full = jnp.broadcast_to(high, vals.shape)
            for h in range(highs):
                masked[pl.ds(h * columns, columns), lanes] = jnp.where(
                    high_full == jnp.bfloat16(h), vals, jnp.bfloat16(0)
                )
        acc[...] += lax.dot_general(
            masked[...], low_hot[...], (((1,), (1,)), ((), ())), preferred_element_type=jnp.float32
        )

    def step(s, carry):
        t = jnp.maximum(s - owns, 0)
        side = lax.rem(t, 2)
        k = lax.div(t, 2)
        is_own = s < owns
        from_below = jnp.logical_and(jnp.logical_not(is_own), jnp.logical_and(side == 0, has_below))
        from_above = jnp.logical_and(jnp.logical_not(is_own), jnp.logical_and(side == 1, has_above))

        @pl.when(from_below)
        def _():
            node_copy(0, k).wait_recv()
            for q in range(fit):
                value_copy(0, k, q).wait_recv()

        @pl.when(from_above)
        def _():
            node_copy(1, k).wait_recv()
            for q in range(fit):
                value_copy(1, k, q).wait_recv()

        @pl.when(jnp.logical_or(is_own, jnp.logical_or(from_below, from_above)))
        def _():
            add_chunk(s)

        return carry

    lax.fori_loop(0, owns + 2 * others, step, 0)

    def pass_flags(step):
        flag_copy(step).wait_recv()
        flags[step + 1] = jnp.maximum(flags[step], flags_in[step])
        if step + 1 < rounds:
            flag_copy(step + 1).start()

    def aside(sweep):
        for step in range(rounds):
            if min(step, SWEEPS - 1) == sweep:
                pass_flags(step)

    halos = (halo_out, halo_in, scale_out, scale_in, hsend_sem, hrecv_sem, ssend_sem, srecv_sem)
    relaxation(acc, fields, weights, halos, surface_stage, smooth_stage, aside)
    full_out[0] = jnp.max(flags[rounds]).astype(jnp.int32)

    for step in range(rounds):
        flag_copy(step).wait_send()
    for side, there in ((0, has_above), (1, has_below)):

        @pl.when(there)
        def _(side=side):
            for k in range(others):
                node_copy(side, k).wait_send()
                for q in range(fit):
                    value_copy(side, k, q).wait_send()


def hand_over(surface, smooth, surface_out, smooth_out, out_sem):
    copies = [
        pltpu.make_async_copy(surface, surface_out, out_sem.at[0]),
        pltpu.make_async_copy(smooth, smooth_out, out_sem.at[1]),
    ]
    for copy in copies:
        copy.start()
    for copy in copies:
        copy.wait()


def body(sensitivity, owner, patch_count, neighbours, coupling):
    columns, faces = sensitivity.shape
    patches = neighbours.shape[0]
    span = patches * NODES
    rows = faces // LANES
    chunk = min(512, faces)
    chunks = faces // chunk
    highs = span // LOW
    hbm = pl.BlockSpec(memory_space=pltpu.HBM)
    vmem = pl.BlockSpec(memory_space=pltpu.VMEM)
    smem = pl.BlockSpec(memory_space=pltpu.SMEM)
    links = neighbours.T.shape
    out = jax.ShapeDtypeStruct((columns, span), jnp.float32)
    kept = pltpu.VMEM((columns, span), jnp.float32)
    dma = pltpu.SemaphoreType.DMA
    operands = (sensitivity, owner.reshape(rows, LANES), patch_count, neighbours.T, coupling.T)
    peers = lax.axis_size("surf")
    link_scratch = [pltpu.VMEM(links, jnp.int32), pltpu.VMEM(links, jnp.float32), dma((2,))]
    field_scratch = [
        pltpu.VMEM((highs * columns, LOW), jnp.float32),
        pltpu.VMEM((SWEEPS, patches + 2 * REACH, columns, NODES), jnp.float32),
        pltpu.VMEM((NOFF + 3, patches, 8, LANES), jnp.float32),
        pltpu.VMEM((16, LANES), jnp.float32),
        *[pltpu.VMEM((2, SWEEPS, columns // GROUP, REACH, GROUP, NODES), jnp.int16)] * 2,
        *[pltpu.VMEM((2, SWEEPS, columns // GROUP, 8, NODES), jnp.float32)] * 2,
    ]

    def hand(outputs):
        return pl.pallas_call(
            hand_over,
            out_shape=(out, out),
            in_specs=[vmem, vmem],
            out_specs=(hbm, hbm),
            scratch_shapes=[dma((2,))],
            compiler_params=pltpu.CompilerParams(vmem_limit_bytes=16 * 1024 * 1024),
        )(*outputs)

    def whole():
        return pl.pallas_call(
            functools.partial(kernel, chunk),
            out_shape=(kept, kept),
            in_specs=[hbm, hbm, smem, hbm, hbm],
            out_specs=(vmem, vmem),
            scratch_shapes=[
                *link_scratch,
                pltpu.VMEM((3, chunks, columns, chunk), jnp.bfloat16),
                pltpu.VMEM((3, rows, LANES), jnp.int32),
                pltpu.VMEM((highs * columns, chunk), jnp.bfloat16),
                pltpu.VMEM((LOW, chunk), jnp.bfloat16),
                *field_scratch,
                dma((2,)),
                dma((chunks,)),
                dma,
                dma((2, chunks)),
                dma((2, chunks)),
                dma((2,)),
                dma((2,)),
                *[dma((2, SWEEPS, columns // GROUP))] * 4,
            ],
            compiler_params=pltpu.CompilerParams(
                collective_id=0, has_side_effects=True, vmem_limit_bytes=VMEM_LIMIT
            ),
        )(*operands)

    if faces % WIDE or highs & (highs - 1) or peers & (peers - 1):
        return hand(whole())

    owns, blocks, fit, rounds = faces // WIDE, faces // BLOCK, WIDE // SLOTS, peers.bit_length() - 1
    others = blocks // fit
    surface, smooth, full = pl.pallas_call(
        packed_kernel,
        out_shape=(kept, kept, jax.ShapeDtypeStruct((1,), jnp.int32)),
        in_specs=[hbm, hbm, smem, hbm, hbm],
        out_specs=(vmem, vmem, smem),
        scratch_shapes=[
            *link_scratch,
            pltpu.VMEM((owns + 2 * others, columns, WIDE), jnp.bfloat16),
            pltpu.VMEM((rows, LANES), jnp.int32),
            pltpu.VMEM((owns + 2 * others, WIDE // LANES, LANES), jnp.int32),
            pltpu.VMEM((2 * rows, LANES), jnp.float32),
            pltpu.VMEM((2, others, columns, WIDE), jnp.bfloat16),
            pltpu.VMEM((2, others, WIDE // LANES, LANES), jnp.int32),
            pltpu.VMEM((2, 2 * SLOTS, BLOCK), jnp.bfloat16),
            pltpu.VMEM((highs * columns, WIDE), jnp.bfloat16),
            pltpu.VMEM((LOW, WIDE), jnp.bfloat16),
            *field_scratch,
            pltpu.VMEM((rounds + 1, 8, LANES), jnp.float32),
            pltpu.VMEM((rounds, 8, LANES), jnp.float32),
            dma((owns,)),
            dma,
            dma((2, others, fit)),
            dma((2, others, fit)),
            dma((2, others)),
            dma((2, others)),
            *[dma((2, SWEEPS, columns // GROUP))] * 4,
            dma((rounds,)),
            dma((rounds,)),
        ],
        compiler_params=pltpu.CompilerParams(collective_id=1, has_side_effects=True, vmem_limit_bytes=VMEM_LIMIT),
    )(*operands)
    _, surface, smooth = lax.while_loop(
        lambda state: state[0] != 0, lambda state: (jnp.int32(0), *hand(whole())), (full[0], *hand((surface, smooth)))
    )
    return surface, smooth


def solution(mesh):
    placed = (
        P(None, ("groups", "surf")),
        P(("groups", "surf")),
        P(("groups", "surf")),
        P(("groups", "surf"), None),
        P(("groups", "surf"), None),
    )
    return jax.shard_map(
        body,
        mesh=mesh,
        in_specs=placed,
        out_specs=(P(None, ("groups", "surf")), P(None, ("groups", "surf"))),
        check_vma=False,
    )
```

```python
import functools

import jax
import jax.numpy as jnp
from jax import lax
from jax.experimental import pallas as pl
from jax.experimental.pallas import tpu as pltpu
from jax.sharding import PartitionSpec as P

NODES = 128
REACH = 4
SWEEPS = 4
LOW = 256
LANES = 128
PAIR = 2
BATCH = 8
BLOCK = 512
SLOTS = 256
WIDE = 1024
DEPTH = REACH * SWEEPS
MARGIN = DEPTH - REACH
GROUP = 48
LEVELS = 32766.0
TINY = 1e-33
VMEM_LIMIT = 60 * 1024 * 1024
smoothing = 1.5
OFFSETS = [d for d in range(-REACH, REACH + 1) if d != 0]
NOFF = len(OFFSETS)
MESH = pl.DeviceIdType.MESH


def tabulate(count, neighbours, coupling, tables):
    patches = neighbours.shape[1]
    position = lax.axis_index("surf")
    slots = lax.broadcasted_iota(jnp.int32, neighbours.shape, 1)
    distance = neighbours[...] - (position * patches + slots)
    links = coupling[...]
    along = lax.broadcasted_iota(jnp.int32, (1, patches), 1)
    alive = jnp.where(along < count[0], 1.0, 0.0).astype(jnp.float32)
    share = alive / (1.0 + smoothing * (2.0 + jnp.sum(links, axis=0, keepdims=True)))
    lines = [
        smoothing * share * jnp.sum(jnp.where(distance == offset, links, 0.0), axis=0, keepdims=True)
        for offset in OFFSETS
    ]
    lines += [share, smoothing * share, alive]
    tables[0] = jnp.zeros(tables.shape[1:], jnp.float32)
    for at, line in enumerate(lines):
        tables[0, pl.ds(at, 1), pl.ds(0, patches)] = line


def table_copy(side, tables, send_sem, recv_sem):
    position = lax.axis_index("surf")
    return pltpu.make_async_remote_copy(
        src_ref=tables.at[0],
        dst_ref=tables.at[1 + side],
        send_sem=send_sem.at[side],
        recv_sem=recv_sem.at[side],
        device_id={"surf": position + 1 if side == 0 else position - 1},
        device_id_type=MESH,
    )


def send_tables(tables, send_sem, recv_sem):
    position = lax.axis_index("surf")

    @pl.when(position < lax.axis_size("surf") - 1)
    def _():
        table_copy(0, tables, send_sem, recv_sem).start()

    @pl.when(position > 0)
    def _():
        table_copy(1, tables, send_sem, recv_sem).start()


def prepare(tables, send_sem, recv_sem, weights, fields):
    patches, columns = fields.shape[1] - 2 * DEPTH, fields.shape[2]
    position = lax.axis_index("surf")
    has_below = position > 0
    has_above = position < lax.axis_size("surf") - 1
    for side, there, landing in ((0, has_below, 0), (1, has_above, patches + DEPTH)):

        @pl.when(there)
        def _(side=side):
            table_copy(side, tables, send_sem, recv_sem).wait_recv()

        @pl.when(jnp.logical_not(there))
        def _(side=side, landing=landing):
            tables[1 + side] = jnp.zeros(tables.shape[1:], jnp.float32)
            fields[0, pl.ds(landing, DEPTH)] = jnp.zeros((DEPTH, columns, NODES), jnp.float32)

    at = lax.broadcasted_iota(jnp.int32, tables.shape[1:], 1)
    below = pltpu.roll(tables[1], (MARGIN - patches) % LANES, 1)
    own = pltpu.roll(tables[0], MARGIN, 1)
    above = pltpu.roll(tables[2], MARGIN + patches, 1)
    count = patches + 2 * MARGIN
    table = jnp.where(at < MARGIN, below, jnp.where(at < MARGIN + patches, own, jnp.where(at < count, above, 0.0)))
    turned = jnp.transpose(table)
    for at in range(NOFF + 3):
        line = jnp.broadcast_to(turned[0:count, at : at + 1], (count, LANES))
        weights[at] = jnp.broadcast_to(line[:, None, :], (count, 8, LANES))


def relaxation(acc, fields, weights, halos, surface_stage, smooth_stage, aside):
    halo_out, halo_in, scale_out, scale_in, hsend_sem, hrecv_sem, ssend_sem, srecv_sem = halos
    columns = fields.shape[2]
    patches = fields.shape[1] - 2 * DEPTH
    highs = patches * NODES // LOW
    groups = columns // GROUP
    position = lax.axis_index("surf")
    has_below = position > 0
    has_above = position < lax.axis_size("surf") - 1

    def halo_copies(side, g, target):
        return [
            pltpu.make_async_remote_copy(
                src_ref=src.at[side, g],
                dst_ref=dst.at[side, g],
                send_sem=send.at[side, g],
                recv_sem=recv.at[side, g],
                device_id={"surf": target},
                device_id_type=MESH,
            )
            for src, dst, send, recv in (
                (scale_out, scale_in, ssend_sem, srecv_sem),
                (halo_out, halo_in, hsend_sem, hrecv_sem),
            )
        ]

    def put_surface(h, g):
        rows = pl.ds(g * GROUP, GROUP)
        for half in range(LOW // NODES):
            p = h * (LOW // NODES) + half
            patch = acc[pl.ds(h * columns + g * GROUP, GROUP), pl.ds(half * NODES, NODES)]
            patch = patch * weights[NOFF + 2, MARGIN + p, 0:1, :]
            fields[0, DEPTH + p, rows] = patch
            surface_stage[rows, pl.ds(p * NODES, NODES)] = patch

    def spread(tile):
        return jnp.concatenate([tile] * (GROUP // 8), axis=0)[None]

    def send_halo(g):
        for side, there, first in ((0, has_above, patches), (1, has_below, DEPTH)):

            @pl.when(there)
            def _(side=side, first=first):
                for part in range(DEPTH // BATCH):
                    patch = fields[0, pl.ds(first + part * BATCH, BATCH), pl.ds(g * GROUP, GROUP)]
                    size = jnp.abs(patch)
                    peak = functools.reduce(
                        jnp.maximum, [size[q, 8 * n : 8 * n + 8] for q in range(BATCH) for n in range(GROUP // 8)]
                    )
                    peak = jnp.maximum(peak, TINY)
                    scale_out[side, g, part] = peak * (1.0 / LEVELS)
                    code = jnp.floor(patch * spread(LEVELS / peak) + 0.5)
                    halo_out[side, g, pl.ds(part * BATCH, BATCH)] = code.astype(jnp.int32).astype(jnp.int16)
                for copy in halo_copies(side, g, position + 1 if side == 0 else position - 1):
                    copy.start()

    def wait_halo(side, g):
        @pl.when(jnp.logical_or(jnp.logical_and(side == 0, has_below), jnp.logical_and(side == 1, has_above)))
        def _():
            for copy in halo_copies(side, g, position - 1 + 2 * side):
                copy.wait_recv()
            for part in range(DEPTH // BATCH):
                code = halo_in[side, g, pl.ds(part * BATCH, BATCH)].astype(jnp.int32).astype(jnp.float32)
                landing = side * (patches + DEPTH) + part * BATCH
                fields[0, pl.ds(landing, BATCH), pl.ds(g * GROUP, GROUP)] = code * spread(scale_in[side, g, part])

    def relax(sweep, g, first):
        for low in range(g * GROUP, (g + 1) * GROUP, 8 * PAIR):
            blocks = [pl.ds(low + 8 * k, 8) for k in range(PAIR)]
            window = [[fields[sweep, first + MARGIN + q, c, :] for q in range(2 * REACH)] for c in blocks]
            for at in range(BATCH):
                p = first + at
                parts = [weights[line, p + MARGIN] for line in range(NOFF + 2)]
                for k, c in enumerate(blocks):
                    window[k].append(fields[sweep, p + DEPTH + REACH, c, :])
                    here = window[k][at + REACH]
                    terms = [parts[line] * window[k][at + REACH + offset] for line, offset in enumerate(OFFSETS)]
                    terms.append(parts[NOFF] * fields[0, p + DEPTH, c, :])
                    terms.append(parts[NOFF + 1] * (pltpu.roll(here, 1, 1) + pltpu.roll(here, NODES - 1, 1)))
                    while len(terms) > 1:
                        terms = [sum(terms[n : n + 2][1:], terms[n]) for n in range(0, len(terms), 2)]
                    if sweep == SWEEPS - 1:
                        smooth_stage[c, pl.ds(pl.multiple_of(p * NODES, NODES), NODES)] = terms[0]
                    else:
                        fields[sweep + 1, p + DEPTH, c, :] = terms[0]

    def relax_range(sweep, g, first, count):
        def one(step, carry):
            relax(sweep, g, first + step * BATCH)
            return carry

        lax.fori_loop(0, count // BATCH, one, 0)

    for g in range(groups):
        for h in range(highs):
            put_surface(h, g)
        send_halo(g)

    for g in range(groups):
        for sweep in range(SWEEPS - 1):
            edge = REACH * (sweep + 1)
            relax_range(sweep, g, edge, patches - 2 * edge)
    aside()

    def turn(at, carry):
        side = lax.rem(position + 1 + at, 2)
        for g in range(groups):
            wait_halo(side, g)
            for sweep in range(SWEEPS):
                low = REACH * sweep - MARGIN
                high = patches - REACH * (sweep + 1)
                relax_range(sweep, g, low + side * (high - low), DEPTH)
        return carry

    lax.fori_loop(0, 2, turn, 0)

    for side, there in ((0, has_above), (1, has_below)):

        @pl.when(there)
        def _(side=side):
            for g in range(groups):
                for copy in halo_copies(side, g, position + 1 if side == 0 else position - 1):
                    copy.wait_send()


def wait_tables(tables, send_sem, recv_sem):
    position = lax.axis_index("surf")

    @pl.when(position < lax.axis_size("surf") - 1)
    def _():
        table_copy(0, tables, send_sem, recv_sem).wait_send()

    @pl.when(position > 0)
    def _():
        table_copy(1, tables, send_sem, recv_sem).wait_send()


def kernel(
    chunk,
    sens,
    owner,
    count,
    neighbours_in,
    coupling_in,
    surface_stage,
    smooth_stage,
    neighbours,
    coupling,
    link_sem,
    values,
    owners,
    masked,
    low_hot,
    acc,
    fields,
    weights,
    tables,
    halo_out,
    halo_in,
    scale_out,
    scale_in,
    out_sem,
    load_sem,
    oload_sem,
    send_sem,
    recv_sem,
    osend_sem,
    orecv_sem,
    hsend_sem,
    hrecv_sem,
    ssend_sem,
    srecv_sem,
    tsend_sem,
    trecv_sem,
):
    columns, faces = sens.shape
    patches = neighbours.shape[1]
    span = patches * NODES
    highs = span // LOW
    chunks = faces // chunk
    pieces = chunk // LANES
    orow = faces // LANES
    position = lax.axis_index("surf")
    peers = lax.axis_size("surf")
    has_below = position > 0
    has_above = position < peers - 1

    def local_load(k):
        return pltpu.make_async_copy(sens.at[:, pl.ds(k * chunk, chunk)], values.at[0, k], load_sem.at[k])

    def face_copy(side, k):
        target = position + 1 if side == 0 else position - 1
        return pltpu.make_async_remote_copy(
            src_ref=sens.at[:, pl.ds(k * chunk, chunk)],
            dst_ref=values.at[1 + side, k],
            send_sem=send_sem.at[side, k],
            recv_sem=recv_sem.at[side, k],
            device_id={"surf": target},
            device_id_type=MESH,
        )

    def owner_copy(side):
        target = position + 1 if side == 0 else position - 1
        return pltpu.make_async_remote_copy(
            src_ref=owner,
            dst_ref=owners.at[1 + side],
            send_sem=osend_sem.at[side],
            recv_sem=orecv_sem.at[side],
            device_id={"surf": target},
            device_id_type=MESH,
        )

    own_owner = pltpu.make_async_copy(owner, owners.at[0], oload_sem)
    own_owner.start()
    link_copies = (
        pltpu.make_async_copy(neighbours_in, neighbours, link_sem.at[0]),
        pltpu.make_async_copy(coupling_in, coupling, link_sem.at[1]),
    )
    for link_copy in link_copies:
        link_copy.start()
    for k in range(chunks):
        local_load(k).start()

    barrier = pltpu.get_barrier_semaphore()

    @pl.when(has_below)
    def _():
        pl.semaphore_signal(barrier, inc=1, device_id={"surf": position - 1}, device_id_type=MESH)

    @pl.when(has_above)
    def _():
        pl.semaphore_signal(barrier, inc=1, device_id={"surf": position + 1}, device_id_type=MESH)

    both = jnp.logical_and(has_below, has_above)

    @pl.when(both)
    def _():
        pl.semaphore_wait(barrier, 2)

    @pl.when(jnp.logical_not(both))
    def _():
        pl.semaphore_wait(barrier, 1)

    @pl.when(has_above)
    def _():
        owner_copy(0).start()

    @pl.when(has_below)
    def _():
        owner_copy(1).start()

    for k in range(chunks):

        @pl.when(has_above)
        def _(k=k):
            face_copy(0, k).start()

        @pl.when(has_below)
        def _(k=k):
            face_copy(1, k).start()

    for link_copy in link_copies:
        link_copy.wait()
    tabulate(count, neighbours, coupling, tables)
    send_tables(tables, tsend_sem, trecv_sem)
    prepare(tables, tsend_sem, trecv_sem, weights, fields)

    acc[...] = jnp.zeros_like(acc)
    first_node = position * span
    low_rows = lax.broadcasted_iota(jnp.int32, (LOW, LANES), 0)

    def add_chunk(slot, k):
        for j in range(pieces):
            local = owners[slot, pl.ds(k * pieces + j, 1), :] - first_node
            high = (local >> 8).astype(jnp.float32).astype(jnp.bfloat16)
            low = local & (LOW - 1)
            lanes = pl.ds(j * LANES, LANES)
            low_hot[:, lanes] = jnp.where(low_rows == low, 1.0, 0.0).astype(jnp.bfloat16)
            vals = values[slot, k, :, lanes]
            high_full = jnp.broadcast_to(high, vals.shape)
            for h in range(highs):
                masked[pl.ds(h * columns, columns), lanes] = jnp.where(
                    high_full == jnp.bfloat16(h), vals, jnp.bfloat16(0)
                )
        acc[...] += lax.dot_general(
            masked[...],
            low_hot[...],
            (((1,), (1,)), ((), ())),
            preferred_element_type=jnp.float32,
        )

    own_owner.wait()

    def step(s, carry):
        is_own = s < chunks
        t = jnp.maximum(s - chunks, 0)
        side = lax.rem(t, 2)
        k = jnp.where(is_own, s, t // 2)
        slot = jnp.where(is_own, 0, 1 + side)

        @pl.when(is_own)
        def _():
            local_load(k).wait()

        from_below = jnp.logical_and(jnp.logical_not(is_own), side == 0)
        from_above = jnp.logical_and(jnp.logical_not(is_own), side == 1)

        @pl.when(jnp.logical_and(from_below, has_below))
        def _():
            @pl.when(t == 0)
            def _():
                owner_copy(0).wait_recv()

            face_copy(0, k).wait_recv()

        @pl.when(jnp.logical_and(from_above, has_above))
        def _():
            @pl.when(t == 1)
            def _():
                owner_copy(1).wait_recv()

            face_copy(1, k).wait_recv()

        present = jnp.logical_or(
            is_own,
            jnp.logical_or(jnp.logical_and(side == 0, has_below), jnp.logical_and(side == 1, has_above)),
        )

        @pl.when(present)
        def _():
            add_chunk(slot, k)

        return carry

    lax.fori_loop(0, 3 * chunks, step, 0)

    halos = (halo_out, halo_in, scale_out, scale_in, hsend_sem, hrecv_sem, ssend_sem, srecv_sem)
    relaxation(acc, fields, weights, halos, surface_stage, smooth_stage, lambda: None)
    wait_tables(tables, tsend_sem, trecv_sem)

    for side, there in ((0, has_above), (1, has_below)):

        @pl.when(there)
        def _(side=side):
            owner_copy(side).wait_send()
            for k in range(chunks):
                face_copy(side, k).wait_send()


def packed_kernel(
    sens,
    owner,
    count,
    neighbours_in,
    coupling_in,
    surface_stage,
    smooth_stage,
    full_out,
    neighbours,
    coupling,
    link_sem,
    values,
    owners,
    nodes,
    spots,
    values_out,
    nodes_out,
    sort_hot,
    masked,
    low_hot,
    acc,
    fields,
    weights,
    tables,
    halo_out,
    halo_in,
    scale_out,
    scale_in,
    flags,
    flags_in,
    load_sem,
    oload_sem,
    send_sem,
    recv_sem,
    nsend_sem,
    nrecv_sem,
    hsend_sem,
    hrecv_sem,
    ssend_sem,
    srecv_sem,
    tsend_sem,
    trecv_sem,
    fsend_sem,
    frecv_sem,
):
    columns, faces = sens.shape
    patches = neighbours.shape[1]
    span = patches * NODES
    highs = span // LOW
    rows = faces // LANES
    owns = faces // WIDE
    blocks = faces // BLOCK
    pieces = WIDE // LANES
    fit = WIDE // SLOTS
    others = blocks // fit
    position = lax.axis_index("surf")
    peers = lax.axis_size("surf")
    rounds = peers.bit_length() - 1
    has_below = position > 0
    has_above = position < peers - 1
    first_node = position * span

    def partner(step):
        size = 2 ** step
        return position + size - 2 * size * (lax.div(position, size) % 2)

    def local_load(k):
        return pltpu.make_async_copy(sens.at[:, pl.ds(k * WIDE, WIDE)], values.at[k], load_sem.at[k])

    def value_copy(side, k, q):
        target = position + 1 if side == 0 else position - 1
        lanes = pl.ds(pl.multiple_of(q * SLOTS, SLOTS), SLOTS)
        return pltpu.make_async_remote_copy(
            src_ref=values_out.at[side, k, :, lanes],
            dst_ref=values.at[owns + 2 * k + side, :, lanes],
            send_sem=send_sem.at[side, k, q],
            recv_sem=recv_sem.at[side, k, q],
            device_id={"surf": target},
            device_id_type=MESH,
        )

    def node_copy(side, k):
        target = position + 1 if side == 0 else position - 1
        return pltpu.make_async_remote_copy(
            src_ref=nodes_out.at[side, k],
            dst_ref=nodes.at[owns + 2 * k + side],
            send_sem=nsend_sem.at[side, k],
            recv_sem=nrecv_sem.at[side, k],
            device_id={"surf": target},
            device_id_type=MESH,
        )

    def flag_copy(step):
        return pltpu.make_async_remote_copy(
            src_ref=flags.at[step],
            dst_ref=flags_in.at[step],
            send_sem=fsend_sem.at[step],
            recv_sem=frecv_sem.at[step],
            device_id={"surf": partner(step)},
            device_id_type=MESH,
        )

    own_owner = pltpu.make_async_copy(owner, owners, oload_sem)
    own_owner.start()
    for k in range(owns):
        local_load(k).start()
    link_copies = (
        pltpu.make_async_copy(neighbours_in, neighbours, link_sem.at[0]),
        pltpu.make_async_copy(coupling_in, coupling, link_sem.at[1]),
    )
    for link_copy in link_copies:
        link_copy.start()

    barrier = pltpu.get_barrier_semaphore()

    @pl.when(has_below)
    def _():
        pl.semaphore_signal(barrier, inc=1, device_id={"surf": position - 1}, device_id_type=MESH)

    @pl.when(has_above)
    def _():
        pl.semaphore_signal(barrier, inc=1, device_id={"surf": position + 1}, device_id_type=MESH)

    for step in range(rounds):
        pl.semaphore_signal(barrier, inc=1, device_id={"surf": partner(step)}, device_id_type=MESH)

    own_owner.wait()
    local = owners[...] - first_node
    for k in range(owns):
        nodes[k] = local[k * pieces : (k + 1) * pieces]
    leaves = jnp.concatenate([local - (span - 1), -local], axis=0) > 0
    marks = jnp.where(leaves, 1.0, 0.0).astype(jnp.bfloat16)
    down = lax.broadcasted_iota(jnp.int32, (LANES, LANES), 0)
    along = lax.broadcasted_iota(jnp.int32, (LANES, LANES), 1)
    earlier = jnp.where(down < along, 1.0, 0.0).astype(jnp.bfloat16)
    block_rows = BLOCK // LANES
    down = lax.broadcasted_iota(jnp.int32, (2 * rows, 2 * rows), 0)
    along = lax.broadcasted_iota(jnp.int32, (2 * rows, 2 * rows), 1)
    same = lax.div(down, block_rows) == lax.div(along, block_rows)
    above = jnp.where(same & (along < down), 1.0, 0.0).astype(jnp.bfloat16)
    sums = jnp.dot(marks, jnp.ones((LANES, LANES), jnp.bfloat16), preferred_element_type=jnp.float32)
    place = jnp.dot(marks, earlier, preferred_element_type=jnp.float32)
    place += jnp.dot(above, sums.astype(jnp.bfloat16), preferred_element_type=jnp.float32)
    spots[...] = jnp.where(leaves, place, 2.0 * SLOTS)
    over = jnp.where(leaves & (place > SLOTS - 0.5), 1.0, 0.0)
    flags[0] = functools.reduce(jnp.maximum, [over[8 * n : 8 * n + 8] for n in range(2 * rows // 8)])

    for link_copy in link_copies:
        link_copy.wait()
    tabulate(count, neighbours, coupling, tables)
    both = jnp.logical_and(has_below, has_above)

    @pl.when(both)
    def _():
        pl.semaphore_wait(barrier, 2 + rounds)

    @pl.when(jnp.logical_not(both))
    def _():
        pl.semaphore_wait(barrier, 1 + rounds)

    flag_copy(0).start()
    send_tables(tables, tsend_sem, trecv_sem)
    for k in range(owns):
        local_load(k).wait()

    slot_rows = lax.broadcasted_iota(jnp.int32, (SLOTS, LANES), 0).astype(jnp.float32).astype(jnp.bfloat16)
    code_rows = lax.broadcasted_iota(jnp.int32, (16, LANES), 0)
    in_wide = WIDE // BLOCK

    def pack(k, carry):
        for q in range(fit):
            at = k * fit + q
            codes = []
            for j in range(block_rows):
                lanes = pl.ds(j * LANES, LANES)
                row = at * block_rows + j
                node = owners[pl.ds(row, 1), :]
                high = jnp.broadcast_to((node >> 8) & (highs - 1), (16, LANES))
                low = jnp.broadcast_to(node & (LOW - 1), (16, LANES))
                code = jnp.where(code_rows == 0, high, jnp.where(code_rows == 1, low, 0))
                codes.append(code.astype(jnp.float32).astype(jnp.bfloat16))
                for side in range(2):
                    spot = spots[pl.ds(side * rows + row, 1), :].astype(jnp.bfloat16)
                    spot = jnp.broadcast_to(spot, (SLOTS, LANES))
                    sort_hot[q % 2, pl.ds(side * SLOTS, SLOTS), lanes] = jnp.where(
                        spot == slot_rows, jnp.bfloat16(1), jnp.bfloat16(0)
                    )
            own = values[k * (fit // in_wide) + q // in_wide, :, pl.ds((q % in_wide) * BLOCK, BLOCK)]
            left = jnp.concatenate([own, jnp.concatenate(codes, axis=1)], axis=0)
            moved = lax.dot_general(
                left, sort_hot[q % 2], (((1,), (1,)), ((), ())), preferred_element_type=jnp.float32
            )
            node = (moved[columns : columns + 1] * LOW + moved[columns + 1 : columns + 2]).astype(jnp.int32)
            for side, there in ((0, has_above), (1, has_below)):
                values_out[side, k, :, pl.ds(q * SLOTS, SLOTS)] = moved[
                    0:columns, side * SLOTS : (side + 1) * SLOTS
                ].astype(jnp.bfloat16)
                for j in range(SLOTS // LANES):
                    nodes_out[side, k, pl.ds(q * (SLOTS // LANES) + j, 1), :] = node[
                        :, side * SLOTS + j * LANES : side * SLOTS + (j + 1) * LANES
                    ]

                @pl.when(there)
                def _(side=side, q=q):
                    value_copy(side, k, q).start()

        for side, there in ((0, has_above), (1, has_below)):

            @pl.when(there)
            def _(side=side):
                node_copy(side, k).start()

        return carry

    lax.fori_loop(0, others, pack, 0)

    acc[...] = jnp.zeros_like(acc)

    def add_chunk(s):
        for j in range(pieces):
            node = nodes[s, pl.ds(j, 1), :]
            high = (node >> 8).astype(jnp.float32).astype(jnp.bfloat16)
            low = (node & (LOW - 1)).astype(jnp.float32).astype(jnp.bfloat16)
            lanes = pl.ds(j * LANES, LANES)
            low_hot[:, lanes] = jnp.where(
                slot_rows == jnp.broadcast_to(low, (LOW, LANES)), jnp.bfloat16(1), jnp.bfloat16(0)
            )
            vals = values[s, :, lanes]
            high_full = jnp.broadcast_to(high, vals.shape)
            for h in range(highs):
                masked[pl.ds(h * columns, columns), lanes] = jnp.where(
                    high_full == jnp.bfloat16(h), vals, jnp.bfloat16(0)
                )
        acc[...] += lax.dot_general(
            masked[...], low_hot[...], (((1,), (1,)), ((), ())), preferred_element_type=jnp.float32
        )

    def pass_flags(step):
        flag_copy(step).wait_recv()
        flags[step + 1] = jnp.maximum(flags[step], flags_in[step])
        if step + 1 < rounds:
            flag_copy(step + 1).start()

    steps = owns + 2 * others
    early = [r for r in range(rounds) if 2 * r + 2 < steps]

    def aside():
        for r in range(len(early), rounds):
            pass_flags(r)

    def step(s, carry):
        t = jnp.maximum(s - owns, 0)
        side = lax.rem(t, 2)
        k = lax.div(t, 2)
        is_own = s < owns
        from_below = jnp.logical_and(jnp.logical_not(is_own), jnp.logical_and(side == 0, has_below))
        from_above = jnp.logical_and(jnp.logical_not(is_own), jnp.logical_and(side == 1, has_above))

        for r in early:

            @pl.when(s == 2 * r + 2)
            def _(r=r):
                pass_flags(r)

        @pl.when(s == owns)
        def _():
            prepare(tables, tsend_sem, trecv_sem, weights, fields)

        @pl.when(from_below)
        def _():
            node_copy(0, k).wait_recv()
            for q in range(fit):
                value_copy(0, k, q).wait_recv()

        @pl.when(from_above)
        def _():
            node_copy(1, k).wait_recv()
            for q in range(fit):
                value_copy(1, k, q).wait_recv()

        @pl.when(jnp.logical_or(is_own, jnp.logical_or(from_below, from_above)))
        def _():
            add_chunk(s)

        return carry

    lax.fori_loop(0, steps, step, 0)

    halos = (halo_out, halo_in, scale_out, scale_in, hsend_sem, hrecv_sem, ssend_sem, srecv_sem)
    relaxation(acc, fields, weights, halos, surface_stage, smooth_stage, aside)
    wait_tables(tables, tsend_sem, trecv_sem)
    full_out[0] = jnp.max(flags[rounds]).astype(jnp.int32)

    for step in range(rounds):
        flag_copy(step).wait_send()
    for side, there in ((0, has_above), (1, has_below)):

        @pl.when(there)
        def _(side=side):
            for k in range(others):
                node_copy(side, k).wait_send()
                for q in range(fit):
                    value_copy(side, k, q).wait_send()


def hand_over(surface, smooth, surface_out, smooth_out, out_sem):
    copies = [
        pltpu.make_async_copy(surface, surface_out, out_sem.at[0]),
        pltpu.make_async_copy(smooth, smooth_out, out_sem.at[1]),
    ]
    for copy in copies:
        copy.start()
    for copy in copies:
        copy.wait()


def body(sensitivity, owner, patch_count, neighbours, coupling):
    columns, faces = sensitivity.shape
    patches = neighbours.shape[0]
    span = patches * NODES
    rows = faces // LANES
    chunk = min(512, faces)
    chunks = faces // chunk
    highs = span // LOW
    hbm = pl.BlockSpec(memory_space=pltpu.HBM)
    vmem = pl.BlockSpec(memory_space=pltpu.VMEM)
    smem = pl.BlockSpec(memory_space=pltpu.SMEM)
    links = neighbours.T.shape
    out = jax.ShapeDtypeStruct((columns, span), jnp.float32)
    kept = pltpu.VMEM((columns, span), jnp.float32)
    dma = pltpu.SemaphoreType.DMA
    operands = (sensitivity, owner.reshape(rows, LANES), patch_count, neighbours.T, coupling.T)
    peers = lax.axis_size("surf")
    link_scratch = [pltpu.VMEM(links, jnp.int32), pltpu.VMEM(links, jnp.float32), dma((2,))]
    field_scratch = [
        pltpu.VMEM((highs * columns, LOW), jnp.float32),
        pltpu.VMEM((SWEEPS, patches + 2 * DEPTH, columns, NODES), jnp.float32),
        pltpu.VMEM((NOFF + 3, patches + 2 * MARGIN, 8, LANES), jnp.float32),
        pltpu.VMEM((3, 16, LANES), jnp.float32),
        *[pltpu.VMEM((2, columns // GROUP, DEPTH, GROUP, NODES), jnp.int16)] * 2,
        *[pltpu.VMEM((2, columns // GROUP, DEPTH // BATCH, 8, NODES), jnp.float32)] * 2,
    ]

    def hand(outputs):
        return pl.pallas_call(
            hand_over,
            out_shape=(out, out),
            in_specs=[vmem, vmem],
            out_specs=(hbm, hbm),
            scratch_shapes=[dma((2,))],
            compiler_params=pltpu.CompilerParams(vmem_limit_bytes=16 * 1024 * 1024),
        )(*outputs)

    def whole():
        return pl.pallas_call(
            functools.partial(kernel, chunk),
            out_shape=(kept, kept),
            in_specs=[hbm, hbm, smem, hbm, hbm],
            out_specs=(vmem, vmem),
            scratch_shapes=[
                *link_scratch,
                pltpu.VMEM((3, chunks, columns, chunk), jnp.bfloat16),
                pltpu.VMEM((3, rows, LANES), jnp.int32),
                pltpu.VMEM((highs * columns, chunk), jnp.bfloat16),
                pltpu.VMEM((LOW, chunk), jnp.bfloat16),
                *field_scratch,
                dma((2,)),
                dma((chunks,)),
                dma,
                dma((2, chunks)),
                dma((2, chunks)),
                dma((2,)),
                dma((2,)),
                *[dma((2, columns // GROUP))] * 4,
            *[dma((2,))] * 2,
            ],
            compiler_params=pltpu.CompilerParams(
                collective_id=0, has_side_effects=True, vmem_limit_bytes=VMEM_LIMIT
            ),
        )(*operands)

    if faces % WIDE or highs & (highs - 1) or peers & (peers - 1):
        return hand(whole())

    owns, blocks, fit, rounds = faces // WIDE, faces // BLOCK, WIDE // SLOTS, peers.bit_length() - 1
    others = blocks // fit
    surface, smooth, full = pl.pallas_call(
        packed_kernel,
        out_shape=(kept, kept, jax.ShapeDtypeStruct((1,), jnp.int32)),
        in_specs=[hbm, hbm, smem, hbm, hbm],
        out_specs=(vmem, vmem, smem),
        scratch_shapes=[
            *link_scratch,
            pltpu.VMEM((owns + 2 * others, columns, WIDE), jnp.bfloat16),
            pltpu.VMEM((rows, LANES), jnp.int32),
            pltpu.VMEM((owns + 2 * others, WIDE // LANES, LANES), jnp.int32),
            pltpu.VMEM((2 * rows, LANES), jnp.float32),
            pltpu.VMEM((2, others, columns, WIDE), jnp.bfloat16),
            pltpu.VMEM((2, others, WIDE // LANES, LANES), jnp.int32),
            pltpu.VMEM((2, 2 * SLOTS, BLOCK), jnp.bfloat16),
            pltpu.VMEM((highs * columns, WIDE), jnp.bfloat16),
            pltpu.VMEM((LOW, WIDE), jnp.bfloat16),
            *field_scratch,
            pltpu.VMEM((rounds + 1, 8, LANES), jnp.float32),
            pltpu.VMEM((rounds, 8, LANES), jnp.float32),
            dma((owns,)),
            dma,
            dma((2, others, fit)),
            dma((2, others, fit)),
            dma((2, others)),
            dma((2, others)),
            *[dma((2, columns // GROUP))] * 4,
            *[dma((2,))] * 2,
            dma((rounds,)),
            dma((rounds,)),
        ],
        compiler_params=pltpu.CompilerParams(collective_id=1, has_side_effects=True, vmem_limit_bytes=VMEM_LIMIT),
    )(*operands)
    _, surface, smooth = lax.while_loop(
        lambda state: state[0] != 0, lambda state: (jnp.int32(0), *hand(whole())), (full[0], *hand((surface, smooth)))
    )
    return surface, smooth


def solution(mesh):
    placed = (
        P(None, ("groups", "surf")),
        P(("groups", "surf")),
        P(("groups", "surf")),
        P(("groups", "surf"), None),
        P(("groups", "surf"), None),
    )
    return jax.shard_map(
        body,
        mesh=mesh,
        in_specs=placed,
        out_specs=(P(None, ("groups", "surf")), P(None, ("groups", "surf"))),
        check_vma=False,
    )
```

```python
import functools

import jax
import jax.numpy as jnp
from jax import lax
from jax.experimental import pallas as pl
from jax.experimental.pallas import tpu as pltpu
from jax.sharding import PartitionSpec as P

NODES = 128
REACH = 4
SWEEPS = 4
LOW = 256
LANES = 128
PAIR = 2
BATCH = 8
BLOCK = 512
SLOTS = 256
WIDE = 1024
DEPTH = REACH * SWEEPS
MARGIN = DEPTH - REACH
GROUP = 48
PART = 8
LEVELS = 32766.0
TINY = 1e-33
VMEM_LIMIT = 60 * 1024 * 1024
smoothing = 1.5
OFFSETS = [d for d in range(-REACH, REACH + 1) if d != 0]
NOFF = len(OFFSETS)
MESH = pl.DeviceIdType.MESH


def tabulate(count, neighbours, coupling, tables):
    patches = neighbours.shape[1]
    position = lax.axis_index("surf")
    slots = lax.broadcasted_iota(jnp.int32, neighbours.shape, 1)
    distance = neighbours[...] - (position * patches + slots)
    links = coupling[...]
    along = lax.broadcasted_iota(jnp.int32, (1, patches), 1)
    alive = jnp.where(along < count[0], 1.0, 0.0).astype(jnp.float32)
    share = alive / (1.0 + smoothing * (2.0 + jnp.sum(links, axis=0, keepdims=True)))
    lines = [
        smoothing * share * jnp.sum(jnp.where(distance == offset, links, 0.0), axis=0, keepdims=True)
        for offset in OFFSETS
    ]
    lines += [share, smoothing * share, alive]
    tables[0] = jnp.zeros(tables.shape[1:], jnp.float32)
    for at, line in enumerate(lines):
        tables[0, pl.ds(at, 1), pl.ds(0, patches)] = line


def table_copy(side, tables, send_sem, recv_sem):
    position = lax.axis_index("surf")
    return pltpu.make_async_remote_copy(
        src_ref=tables.at[0],
        dst_ref=tables.at[1 + side],
        send_sem=send_sem.at[side],
        recv_sem=recv_sem.at[side],
        device_id={"surf": position + 1 if side == 0 else position - 1},
        device_id_type=MESH,
    )


def send_tables(tables, send_sem, recv_sem):
    position = lax.axis_index("surf")

    @pl.when(position < lax.axis_size("surf") - 1)
    def _():
        table_copy(0, tables, send_sem, recv_sem).start()

    @pl.when(position > 0)
    def _():
        table_copy(1, tables, send_sem, recv_sem).start()


def prepare(tables, send_sem, recv_sem, weights, fields):
    patches, columns = fields.shape[1] - 2 * DEPTH, fields.shape[2]
    position = lax.axis_index("surf")
    has_below = position > 0
    has_above = position < lax.axis_size("surf") - 1
    for side, there, landing in ((0, has_below, 0), (1, has_above, patches + DEPTH)):

        @pl.when(there)
        def _(side=side):
            table_copy(side, tables, send_sem, recv_sem).wait_recv()

        @pl.when(jnp.logical_not(there))
        def _(side=side, landing=landing):
            tables[1 + side] = jnp.zeros(tables.shape[1:], jnp.float32)
            fields[0, pl.ds(landing, DEPTH)] = jnp.zeros((DEPTH, columns, NODES), jnp.float32)

    at = lax.broadcasted_iota(jnp.int32, tables.shape[1:], 1)
    below = pltpu.roll(tables[1], (MARGIN - patches) % LANES, 1)
    own = pltpu.roll(tables[0], MARGIN, 1)
    above = pltpu.roll(tables[2], MARGIN + patches, 1)
    count = patches + 2 * MARGIN
    table = jnp.where(at < MARGIN, below, jnp.where(at < MARGIN + patches, own, jnp.where(at < count, above, 0.0)))
    turned = jnp.transpose(table)
    for at in range(NOFF + 3):
        line = jnp.broadcast_to(turned[0:count, at : at + 1], (count, LANES))
        weights[at] = jnp.broadcast_to(line[:, None, :], (count, 8, LANES))


def relaxation(acc, fields, weights, halos, surface_stage, smooth_stage, gather, aside):
    halo_out, halo_in, scale_out, scale_in, hsend_sem, hrecv_sem, ssend_sem, srecv_sem = halos
    columns = fields.shape[2]
    patches = fields.shape[1] - 2 * DEPTH
    highs = patches * NODES // LOW
    groups = columns // GROUP
    position = lax.axis_index("surf")
    has_below = position > 0
    has_above = position < lax.axis_size("surf") - 1

    def halo_copies(side, g, target):
        return [
            pltpu.make_async_remote_copy(
                src_ref=src.at[side, g],
                dst_ref=dst.at[side, g],
                send_sem=send.at[side, g],
                recv_sem=recv.at[side, g],
                device_id={"surf": target},
                device_id_type=MESH,
            )
            for src, dst, send, recv in (
                (scale_out, scale_in, ssend_sem, srecv_sem),
                (halo_out, halo_in, hsend_sem, hrecv_sem),
            )
        ]

    def put_surface(h, g):
        rows = pl.ds(g * GROUP, GROUP)
        for half in range(LOW // NODES):
            p = h * (LOW // NODES) + half
            patch = acc[pl.ds(pl.multiple_of((g * highs + h) * GROUP, 8), GROUP), pl.ds(half * NODES, NODES)]
            patch = patch * weights[NOFF + 2, MARGIN + p, 0:1, :]
            fields[0, DEPTH + p, rows] = patch
            surface_stage[rows, pl.ds(pl.multiple_of(p * NODES, NODES), NODES)] = patch

    def spread(tile):
        return jnp.concatenate([tile] * (GROUP // 8), axis=0)[None]

    def send_halo(side, g):
        @pl.when(jnp.logical_or(jnp.logical_and(side == 0, has_above), jnp.logical_and(side == 1, has_below)))
        def _():
            first = patches + side * (DEPTH - patches)
            for part in range(DEPTH // PART):
                patch = fields[0, pl.ds(first + part * PART, PART), pl.ds(g * GROUP, GROUP)]
                size = jnp.abs(patch)
                peak = functools.reduce(
                    jnp.maximum, [size[q, 8 * n : 8 * n + 8] for q in range(PART) for n in range(GROUP // 8)]
                )
                peak = jnp.maximum(peak, TINY)
                scale_out[side, g, part] = peak * (1.0 / LEVELS)
                code = jnp.floor(patch * spread(LEVELS / peak) + 0.5)
                halo_out[side, g, pl.ds(part * PART, PART)] = code.astype(jnp.int32).astype(jnp.int16)
            for copy in halo_copies(side, g, position + 1 - 2 * side):
                copy.start()

    def wait_halo(side, g):
        @pl.when(jnp.logical_or(jnp.logical_and(side == 0, has_below), jnp.logical_and(side == 1, has_above)))
        def _():
            for copy in halo_copies(side, g, position - 1 + 2 * side):
                copy.wait_recv()
            for part in range(DEPTH // PART):
                code = halo_in[side, g, pl.ds(part * PART, PART)].astype(jnp.int32).astype(jnp.float32)
                landing = side * (patches + DEPTH) + part * PART
                fields[0, pl.ds(landing, PART), pl.ds(g * GROUP, GROUP)] = code * spread(scale_in[side, g, part])

    def relax(sweep, g, first):
        for low in range(g * GROUP, (g + 1) * GROUP, 8 * PAIR):
            blocks = [pl.ds(low + 8 * k, 8) for k in range(PAIR)]
            window = [[fields[sweep, first + MARGIN + q, c, :] for q in range(2 * REACH)] for c in blocks]
            for at in range(BATCH):
                p = first + at
                parts = [weights[line, p + MARGIN] for line in range(NOFF + 2)]
                for k, c in enumerate(blocks):
                    window[k].append(fields[sweep, p + DEPTH + REACH, c, :])
                    here = window[k][at + REACH]
                    terms = [parts[line] * window[k][at + REACH + offset] for line, offset in enumerate(OFFSETS)]
                    terms.append(parts[NOFF] * fields[0, p + DEPTH, c, :])
                    terms.append(parts[NOFF + 1] * (pltpu.roll(here, 1, 1) + pltpu.roll(here, NODES - 1, 1)))
                    while len(terms) > 1:
                        terms = [sum(terms[n : n + 2][1:], terms[n]) for n in range(0, len(terms), 2)]
                    if sweep == SWEEPS - 1:
                        smooth_stage[c, pl.ds(pl.multiple_of(p * NODES, NODES), NODES)] = terms[0]
                    else:
                        fields[sweep + 1, p + DEPTH, c, :] = terms[0]

    def relax_range(sweep, g, first, count):
        def one(step, carry):
            relax(sweep, g, first + step * BATCH)
            return carry

        lax.fori_loop(0, count // BATCH, one, 0)

    ends = DEPTH * NODES // LOW

    for g in range(groups):
        gather(g)

        def leave(at, carry, g=g):
            side = lax.rem(position + 1 + at, 2)
            for h in range(ends):
                put_surface(h + (1 - side) * (highs - ends), g)
            send_halo(side, g)
            return carry

        lax.fori_loop(0, 2, leave, 0)
    for g in range(groups):
        for h in range(ends, highs - ends):
            put_surface(h, g)

    for g in range(groups):
        for sweep in range(SWEEPS - 1):
            edge = REACH * (sweep + 1)
            relax_range(sweep, g, edge, patches - 2 * edge)
    aside()

    def turn(at, carry):
        side = lax.rem(position + 1 + at, 2)
        for g in range(groups):
            wait_halo(side, g)
            for sweep in range(SWEEPS):
                low = REACH * sweep - MARGIN
                high = patches - REACH * (sweep + 1)
                relax_range(sweep, g, low + side * (high - low), DEPTH)
        return carry

    lax.fori_loop(0, 2, turn, 0)

    for side, there in ((0, has_above), (1, has_below)):

        @pl.when(there)
        def _(side=side):
            for g in range(groups):
                for copy in halo_copies(side, g, position + 1 if side == 0 else position - 1):
                    copy.wait_send()


def wait_tables(tables, send_sem, recv_sem):
    position = lax.axis_index("surf")

    @pl.when(position < lax.axis_size("surf") - 1)
    def _():
        table_copy(0, tables, send_sem, recv_sem).wait_send()

    @pl.when(position > 0)
    def _():
        table_copy(1, tables, send_sem, recv_sem).wait_send()


def kernel(
    chunk,
    sens,
    owner,
    count,
    neighbours_in,
    coupling_in,
    surface_stage,
    smooth_stage,
    neighbours,
    coupling,
    link_sem,
    values,
    owners,
    masked,
    low_hot,
    acc,
    fields,
    weights,
    tables,
    halo_out,
    halo_in,
    scale_out,
    scale_in,
    out_sem,
    load_sem,
    oload_sem,
    send_sem,
    recv_sem,
    osend_sem,
    orecv_sem,
    hsend_sem,
    hrecv_sem,
    ssend_sem,
    srecv_sem,
    tsend_sem,
    trecv_sem,
):
    columns, faces = sens.shape
    patches = neighbours.shape[1]
    span = patches * NODES
    highs = span // LOW
    chunks = faces // chunk
    pieces = chunk // LANES
    orow = faces // LANES
    position = lax.axis_index("surf")
    peers = lax.axis_size("surf")
    has_below = position > 0
    has_above = position < peers - 1

    def local_load(k):
        return pltpu.make_async_copy(sens.at[:, pl.ds(k * chunk, chunk)], values.at[0, k], load_sem.at[k])

    def face_copy(side, k):
        target = position + 1 if side == 0 else position - 1
        return pltpu.make_async_remote_copy(
            src_ref=sens.at[:, pl.ds(k * chunk, chunk)],
            dst_ref=values.at[1 + side, k],
            send_sem=send_sem.at[side, k],
            recv_sem=recv_sem.at[side, k],
            device_id={"surf": target},
            device_id_type=MESH,
        )

    def owner_copy(side):
        target = position + 1 if side == 0 else position - 1
        return pltpu.make_async_remote_copy(
            src_ref=owner,
            dst_ref=owners.at[1 + side],
            send_sem=osend_sem.at[side],
            recv_sem=orecv_sem.at[side],
            device_id={"surf": target},
            device_id_type=MESH,
        )

    own_owner = pltpu.make_async_copy(owner, owners.at[0], oload_sem)
    own_owner.start()
    link_copies = (
        pltpu.make_async_copy(neighbours_in, neighbours, link_sem.at[0]),
        pltpu.make_async_copy(coupling_in, coupling, link_sem.at[1]),
    )
    for link_copy in link_copies:
        link_copy.start()
    for k in range(chunks):
        local_load(k).start()

    barrier = pltpu.get_barrier_semaphore()

    @pl.when(has_below)
    def _():
        pl.semaphore_signal(barrier, inc=1, device_id={"surf": position - 1}, device_id_type=MESH)

    @pl.when(has_above)
    def _():
        pl.semaphore_signal(barrier, inc=1, device_id={"surf": position + 1}, device_id_type=MESH)

    both = jnp.logical_and(has_below, has_above)

    @pl.when(both)
    def _():
        pl.semaphore_wait(barrier, 2)

    @pl.when(jnp.logical_not(both))
    def _():
        pl.semaphore_wait(barrier, 1)

    @pl.when(has_above)
    def _():
        owner_copy(0).start()

    @pl.when(has_below)
    def _():
        owner_copy(1).start()

    for k in range(chunks):

        @pl.when(has_above)
        def _(k=k):
            face_copy(0, k).start()

        @pl.when(has_below)
        def _(k=k):
            face_copy(1, k).start()

    for link_copy in link_copies:
        link_copy.wait()
    tabulate(count, neighbours, coupling, tables)
    send_tables(tables, tsend_sem, trecv_sem)
    prepare(tables, tsend_sem, trecv_sem, weights, fields)

    acc[...] = jnp.zeros_like(acc)
    first_node = position * span
    low_rows = lax.broadcasted_iota(jnp.int32, (LOW, LANES), 0)

    def add_chunk(slot, k):
        for j in range(pieces):
            local = owners[slot, pl.ds(k * pieces + j, 1), :] - first_node
            high = (local >> 8).astype(jnp.float32).astype(jnp.bfloat16)
            low = local & (LOW - 1)
            lanes = pl.ds(j * LANES, LANES)
            low_hot[:, lanes] = jnp.where(low_rows == low, 1.0, 0.0).astype(jnp.bfloat16)
            vals = values[slot, k, :, lanes]
            high_full = jnp.broadcast_to(high, vals.shape)
            for h in range(highs):
                kept = jnp.where(high_full == jnp.bfloat16(h), vals, jnp.bfloat16(0))
                for g in range(columns // GROUP):
                    masked[pl.ds((g * highs + h) * GROUP, GROUP), lanes] = kept[g * GROUP : (g + 1) * GROUP]
        acc[...] += lax.dot_general(
            masked[...],
            low_hot[...],
            (((1,), (1,)), ((), ())),
            preferred_element_type=jnp.float32,
        )

    own_owner.wait()

    def step(s, carry):
        is_own = s < chunks
        t = jnp.maximum(s - chunks, 0)
        side = lax.rem(t, 2)
        k = jnp.where(is_own, s, t // 2)
        slot = jnp.where(is_own, 0, 1 + side)

        @pl.when(is_own)
        def _():
            local_load(k).wait()

        from_below = jnp.logical_and(jnp.logical_not(is_own), side == 0)
        from_above = jnp.logical_and(jnp.logical_not(is_own), side == 1)

        @pl.when(jnp.logical_and(from_below, has_below))
        def _():
            @pl.when(t == 0)
            def _():
                owner_copy(0).wait_recv()

            face_copy(0, k).wait_recv()

        @pl.when(jnp.logical_and(from_above, has_above))
        def _():
            @pl.when(t == 1)
            def _():
                owner_copy(1).wait_recv()

            face_copy(1, k).wait_recv()

        present = jnp.logical_or(
            is_own,
            jnp.logical_or(jnp.logical_and(side == 0, has_below), jnp.logical_and(side == 1, has_above)),
        )

        @pl.when(present)
        def _():
            add_chunk(slot, k)

        return carry

    lax.fori_loop(0, 3 * chunks, step, 0)

    halos = (halo_out, halo_in, scale_out, scale_in, hsend_sem, hrecv_sem, ssend_sem, srecv_sem)
    relaxation(acc, fields, weights, halos, surface_stage, smooth_stage, lambda g: None, lambda: None)
    wait_tables(tables, tsend_sem, trecv_sem)

    for side, there in ((0, has_above), (1, has_below)):

        @pl.when(there)
        def _(side=side):
            owner_copy(side).wait_send()
            for k in range(chunks):
                face_copy(side, k).wait_send()


def flag_masks(peers):
    bits = peers.bit_length() - 1
    return [[mask << at for mask in ((1, 2, 3) if at + 1 < bits else (1,))] for at in range(0, bits, 2)]


def packed_kernel(
    sens,
    owner,
    count,
    neighbours_in,
    coupling_in,
    surface_stage,
    smooth_stage,
    full_out,
    neighbours,
    coupling,
    link_sem,
    values,
    owners,
    nodes,
    spots,
    values_out,
    nodes_out,
    sort_hot,
    masked,
    low_hot,
    acc,
    fields,
    weights,
    tables,
    halo_out,
    halo_in,
    scale_out,
    scale_in,
    flags,
    flags_in,
    load_sem,
    oload_sem,
    send_sem,
    recv_sem,
    nsend_sem,
    nrecv_sem,
    hsend_sem,
    hrecv_sem,
    ssend_sem,
    srecv_sem,
    tsend_sem,
    trecv_sem,
    fsend_sem,
    frecv_sem,
):
    columns, faces = sens.shape
    patches = neighbours.shape[1]
    span = patches * NODES
    highs = span // LOW
    rows = faces // LANES
    owns = faces // WIDE
    blocks = faces // BLOCK
    pieces = WIDE // LANES
    fit = WIDE // SLOTS
    others = blocks // fit
    groups = columns // GROUP
    position = lax.axis_index("surf")
    peers = lax.axis_size("surf")
    masks = flag_masks(peers)
    has_below = position > 0
    has_above = position < peers - 1
    first_node = position * span

    def partner(mask):
        other = position
        for bit in range(peers.bit_length()):
            size = 2**bit
            if mask & size:
                other = other + size - 2 * size * (lax.div(position, size) % 2)
        return other

    def local_load(k):
        return pltpu.make_async_copy(sens.at[:, pl.ds(k * WIDE, WIDE)], values.at[k], load_sem.at[k])

    def value_copy(side, k, q, g):
        target = position + 1 if side == 0 else position - 1
        lanes = pl.ds(pl.multiple_of(q * SLOTS, SLOTS), SLOTS)
        return pltpu.make_async_remote_copy(
            src_ref=values_out.at[side, k, pl.ds(g * GROUP, GROUP), lanes],
            dst_ref=values.at[owns + 2 * k + side, pl.ds(g * GROUP, GROUP), lanes],
            send_sem=send_sem.at[side, k, q, g],
            recv_sem=recv_sem.at[side, k, q, g],
            device_id={"surf": target},
            device_id_type=MESH,
        )

    def node_copy(side, k):
        target = position + 1 if side == 0 else position - 1
        return pltpu.make_async_remote_copy(
            src_ref=nodes_out.at[side, k],
            dst_ref=nodes.at[owns + 2 * k + side],
            send_sem=nsend_sem.at[side, k],
            recv_sem=nrecv_sem.at[side, k],
            device_id={"surf": target},
            device_id_type=MESH,
        )

    def flag_copies(step):
        return [
            pltpu.make_async_remote_copy(
                src_ref=flags.at[step],
                dst_ref=flags_in.at[step, n],
                send_sem=fsend_sem.at[step, n],
                recv_sem=frecv_sem.at[step, n],
                device_id={"surf": partner(mask)},
                device_id_type=MESH,
            )
            for n, mask in enumerate(masks[step])
        ]

    own_owner = pltpu.make_async_copy(owner, owners, oload_sem)
    own_owner.start()
    for k in range(owns):
        local_load(k).start()
    link_copies = (
        pltpu.make_async_copy(neighbours_in, neighbours, link_sem.at[0]),
        pltpu.make_async_copy(coupling_in, coupling, link_sem.at[1]),
    )
    for link_copy in link_copies:
        link_copy.start()

    barrier = pltpu.get_barrier_semaphore()

    @pl.when(has_below)
    def _():
        pl.semaphore_signal(barrier, inc=1, device_id={"surf": position - 1}, device_id_type=MESH)

    @pl.when(has_above)
    def _():
        pl.semaphore_signal(barrier, inc=1, device_id={"surf": position + 1}, device_id_type=MESH)

    greeted = [mask for step in masks for mask in step]
    for mask in greeted:
        pl.semaphore_signal(barrier, inc=1, device_id={"surf": partner(mask)}, device_id_type=MESH)

    own_owner.wait()
    local = owners[...] - first_node
    for k in range(owns):
        nodes[k] = local[k * pieces : (k + 1) * pieces]
    leaves = jnp.concatenate([local - (span - 1), -local], axis=0) > 0
    marks = jnp.where(leaves, 1.0, 0.0).astype(jnp.bfloat16)
    down = lax.broadcasted_iota(jnp.int32, (LANES, LANES), 0)
    along = lax.broadcasted_iota(jnp.int32, (LANES, LANES), 1)
    earlier = jnp.where(down < along, 1.0, 0.0).astype(jnp.bfloat16)
    block_rows = BLOCK // LANES
    down = lax.broadcasted_iota(jnp.int32, (2 * rows, 2 * rows), 0)
    along = lax.broadcasted_iota(jnp.int32, (2 * rows, 2 * rows), 1)
    same = lax.div(down, block_rows) == lax.div(along, block_rows)
    above = jnp.where(same & (along < down), 1.0, 0.0).astype(jnp.bfloat16)
    sums = jnp.dot(marks, jnp.ones((LANES, LANES), jnp.bfloat16), preferred_element_type=jnp.float32)
    place = jnp.dot(marks, earlier, preferred_element_type=jnp.float32)
    place += jnp.dot(above, sums.astype(jnp.bfloat16), preferred_element_type=jnp.float32)
    spots[...] = jnp.where(leaves, place, 2.0 * SLOTS)
    over = jnp.where(leaves & (place > SLOTS - 0.5), 1.0, 0.0)
    flags[0] = functools.reduce(jnp.maximum, [over[8 * n : 8 * n + 8] for n in range(2 * rows // 8)])

    for link_copy in link_copies:
        link_copy.wait()
    tabulate(count, neighbours, coupling, tables)
    both = jnp.logical_and(has_below, has_above)

    @pl.when(both)
    def _():
        pl.semaphore_wait(barrier, 2 + len(greeted))

    @pl.when(jnp.logical_not(both))
    def _():
        pl.semaphore_wait(barrier, 1 + len(greeted))

    for copy in flag_copies(0):
        copy.start()
    send_tables(tables, tsend_sem, trecv_sem)
    for k in range(owns):
        local_load(k).wait()

    slot_rows = lax.broadcasted_iota(jnp.int32, (SLOTS, LANES), 0).astype(jnp.float32).astype(jnp.bfloat16)
    code_rows = lax.broadcasted_iota(jnp.int32, (16, LANES), 0)
    in_wide = WIDE // BLOCK

    def pack(k, carry):
        for q in range(fit):
            at = k * fit + q
            codes = []
            for j in range(block_rows):
                lanes = pl.ds(j * LANES, LANES)
                row = at * block_rows + j
                node = owners[pl.ds(row, 1), :]
                high = jnp.broadcast_to((node >> 8) & (highs - 1), (16, LANES))
                low = jnp.broadcast_to(node & (LOW - 1), (16, LANES))
                code = jnp.where(code_rows == 0, high, jnp.where(code_rows == 1, low, 0))
                codes.append(code.astype(jnp.float32).astype(jnp.bfloat16))
                for side in range(2):
                    spot = spots[pl.ds(side * rows + row, 1), :].astype(jnp.bfloat16)
                    spot = jnp.broadcast_to(spot, (SLOTS, LANES))
                    sort_hot[q % 2, pl.ds(side * SLOTS, SLOTS), lanes] = jnp.where(
                        spot == slot_rows, jnp.bfloat16(1), jnp.bfloat16(0)
                    )
            own = values[k * (fit // in_wide) + q // in_wide, :, pl.ds((q % in_wide) * BLOCK, BLOCK)]
            left = jnp.concatenate([own, jnp.concatenate(codes, axis=1)], axis=0)
            moved = lax.dot_general(
                left, sort_hot[q % 2], (((1,), (1,)), ((), ())), preferred_element_type=jnp.float32
            )
            node = (moved[columns : columns + 1] * LOW + moved[columns + 1 : columns + 2]).astype(jnp.int32)
            for side, there in ((0, has_above), (1, has_below)):
                values_out[side, k, :, pl.ds(q * SLOTS, SLOTS)] = moved[
                    0:columns, side * SLOTS : (side + 1) * SLOTS
                ].astype(jnp.bfloat16)
                for j in range(SLOTS // LANES):
                    nodes_out[side, k, pl.ds(q * (SLOTS // LANES) + j, 1), :] = node[
                        :, side * SLOTS + j * LANES : side * SLOTS + (j + 1) * LANES
                    ]

                @pl.when(there)
                def _(side=side, q=q):
                    value_copy(side, k, q, 0).start()

        for side, there in ((0, has_above), (1, has_below)):

            @pl.when(there)
            def _(side=side):
                node_copy(side, k).start()

        return carry

    lax.fori_loop(0, others, pack, 0)

    def send_more(k, carry):
        for side, there in ((0, has_above), (1, has_below)):

            @pl.when(there)
            def _(side=side):
                for g in range(1, groups):
                    for q in range(fit):
                        value_copy(side, k, q, g).start()

        return carry

    lax.fori_loop(0, others, send_more, 0)

    acc[...] = jnp.zeros_like(acc)

    def add_chunk(s, g):
        for j in range(pieces):
            node = nodes[s, pl.ds(j, 1), :]
            high = (node >> 8).astype(jnp.float32).astype(jnp.bfloat16)
            low = (node & (LOW - 1)).astype(jnp.float32).astype(jnp.bfloat16)
            lanes = pl.ds(j * LANES, LANES)
            low_hot[:, lanes] = jnp.where(
                slot_rows == jnp.broadcast_to(low, (LOW, LANES)), jnp.bfloat16(1), jnp.bfloat16(0)
            )
            vals = values[s, pl.ds(g * GROUP, GROUP), lanes]
            high_full = jnp.broadcast_to(high, vals.shape)
            for h in range(highs):
                masked[pl.ds(h * GROUP, GROUP), lanes] = jnp.where(
                    high_full == jnp.bfloat16(h), vals, jnp.bfloat16(0)
                )
        acc[pl.ds(g * highs * GROUP, highs * GROUP)] += lax.dot_general(
            masked[...], low_hot[...], (((1,), (1,)), ((), ())), preferred_element_type=jnp.float32
        )

    def pass_flags(step):
        total = flags[step]
        for n, copy in enumerate(flag_copies(step)):
            copy.wait_recv()
            total = jnp.maximum(total, flags_in[step, n])
        flags[step + 1] = total
        if step + 1 < len(masks):
            for copy in flag_copies(step + 1):
                copy.start()

    def aside():
        for step in range(1, len(masks) - 1):
            pass_flags(step)

    def step(g, s, carry):
        t = jnp.maximum(s - owns, 0)
        side = lax.rem(position + 1 + lax.div(t, others), 2)
        k = lax.rem(t, others)
        is_own = s < owns
        slot = jnp.where(is_own, s, owns + 2 * k + side)
        from_below = jnp.logical_and(jnp.logical_not(is_own), jnp.logical_and(side == 0, has_below))
        from_above = jnp.logical_and(jnp.logical_not(is_own), jnp.logical_and(side == 1, has_above))

        if g == 0:

            @pl.when(s == owns)
            def _():
                if len(masks) > 1:
                    pass_flags(0)
                prepare(tables, tsend_sem, trecv_sem, weights, fields)

        @pl.when(from_below)
        def _():
            if g == 0:
                node_copy(0, k).wait_recv()
            for q in range(fit):
                value_copy(0, k, q, g).wait_recv()

        @pl.when(from_above)
        def _():
            if g == 0:
                node_copy(1, k).wait_recv()
            for q in range(fit):
                value_copy(1, k, q, g).wait_recv()

        @pl.when(jnp.logical_or(is_own, jnp.logical_or(from_below, from_above)))
        def _():
            add_chunk(slot, g)

        return carry

    def gather(g):
        lax.fori_loop(0, owns + 2 * others, functools.partial(step, g), 0)

    halos = (halo_out, halo_in, scale_out, scale_in, hsend_sem, hrecv_sem, ssend_sem, srecv_sem)
    relaxation(acc, fields, weights, halos, surface_stage, smooth_stage, gather, aside)
    wait_tables(tables, tsend_sem, trecv_sem)
    pass_flags(len(masks) - 1)
    full_out[0] = jnp.max(flags[len(masks)]).astype(jnp.int32)

    for step in range(len(masks)):
        for copy in flag_copies(step):
            copy.wait_send()
    for side, there in ((0, has_above), (1, has_below)):

        @pl.when(there)
        def _(side=side):
            for k in range(others):
                node_copy(side, k).wait_send()
                for q in range(fit):
                    for g in range(groups):
                        value_copy(side, k, q, g).wait_send()


def hand_over(surface, smooth, surface_out, smooth_out, out_sem):
    copies = [
        pltpu.make_async_copy(surface, surface_out, out_sem.at[0]),
        pltpu.make_async_copy(smooth, smooth_out, out_sem.at[1]),
    ]
    for copy in copies:
        copy.start()
    for copy in copies:
        copy.wait()


def body(sensitivity, owner, patch_count, neighbours, coupling):
    columns, faces = sensitivity.shape
    patches = neighbours.shape[0]
    span = patches * NODES
    rows = faces // LANES
    chunk = min(512, faces)
    chunks = faces // chunk
    highs = span // LOW
    hbm = pl.BlockSpec(memory_space=pltpu.HBM)
    vmem = pl.BlockSpec(memory_space=pltpu.VMEM)
    smem = pl.BlockSpec(memory_space=pltpu.SMEM)
    links = neighbours.T.shape
    out = jax.ShapeDtypeStruct((columns, span), jnp.float32)
    kept = pltpu.VMEM((columns, span), jnp.float32)
    dma = pltpu.SemaphoreType.DMA
    operands = (sensitivity, owner.reshape(rows, LANES), patch_count, neighbours.T, coupling.T)
    peers = lax.axis_size("surf")
    link_scratch = [pltpu.VMEM(links, jnp.int32), pltpu.VMEM(links, jnp.float32), dma((2,))]
    field_scratch = [
        pltpu.VMEM((highs * columns, LOW), jnp.float32),
        pltpu.VMEM((SWEEPS, patches + 2 * DEPTH, columns, NODES), jnp.float32),
        pltpu.VMEM((NOFF + 3, patches + 2 * MARGIN, 8, LANES), jnp.float32),
        pltpu.VMEM((3, 16, LANES), jnp.float32),
        *[pltpu.VMEM((2, columns // GROUP, DEPTH, GROUP, NODES), jnp.int16)] * 2,
        *[pltpu.VMEM((2, columns // GROUP, DEPTH // PART, 8, NODES), jnp.float32)] * 2,
    ]

    def hand(outputs):
        return pl.pallas_call(
            hand_over,
            out_shape=(out, out),
            in_specs=[vmem, vmem],
            out_specs=(hbm, hbm),
            scratch_shapes=[dma((2,))],
            compiler_params=pltpu.CompilerParams(vmem_limit_bytes=16 * 1024 * 1024),
        )(*outputs)

    def whole():
        return pl.pallas_call(
            functools.partial(kernel, chunk),
            out_shape=(kept, kept),
            in_specs=[hbm, hbm, smem, hbm, hbm],
            out_specs=(vmem, vmem),
            scratch_shapes=[
                *link_scratch,
                pltpu.VMEM((3, chunks, columns, chunk), jnp.bfloat16),
                pltpu.VMEM((3, rows, LANES), jnp.int32),
                pltpu.VMEM((highs * columns, chunk), jnp.bfloat16),
                pltpu.VMEM((LOW, chunk), jnp.bfloat16),
                *field_scratch,
                dma((2,)),
                dma((chunks,)),
                dma,
                dma((2, chunks)),
                dma((2, chunks)),
                dma((2,)),
                dma((2,)),
                *[dma((2, columns // GROUP))] * 4,
            *[dma((2,))] * 2,
            ],
            compiler_params=pltpu.CompilerParams(
                collective_id=0, has_side_effects=True, vmem_limit_bytes=VMEM_LIMIT
            ),
        )(*operands)

    if faces % WIDE or highs & (highs - 1) or peers & (peers - 1) or peers < 2:
        return hand(whole())

    owns, blocks, fit, rounds = faces // WIDE, faces // BLOCK, WIDE // SLOTS, len(flag_masks(peers))
    others = blocks // fit
    surface, smooth, full = pl.pallas_call(
        packed_kernel,
        out_shape=(kept, kept, jax.ShapeDtypeStruct((1,), jnp.int32)),
        in_specs=[hbm, hbm, smem, hbm, hbm],
        out_specs=(vmem, vmem, smem),
        scratch_shapes=[
            *link_scratch,
            pltpu.VMEM((owns + 2 * others, columns, WIDE), jnp.bfloat16),
            pltpu.VMEM((rows, LANES), jnp.int32),
            pltpu.VMEM((owns + 2 * others, WIDE // LANES, LANES), jnp.int32),
            pltpu.VMEM((2 * rows, LANES), jnp.float32),
            pltpu.VMEM((2, others, columns, WIDE), jnp.bfloat16),
            pltpu.VMEM((2, others, WIDE // LANES, LANES), jnp.int32),
            pltpu.VMEM((2, 2 * SLOTS, BLOCK), jnp.bfloat16),
            pltpu.VMEM((highs * GROUP, WIDE), jnp.bfloat16),
            pltpu.VMEM((LOW, WIDE), jnp.bfloat16),
            *field_scratch,
            pltpu.VMEM((rounds + 1, 8, LANES), jnp.float32),
            pltpu.VMEM((rounds, 3, 8, LANES), jnp.float32),
            dma((owns,)),
            dma,
            dma((2, others, fit, columns // GROUP)),
            dma((2, others, fit, columns // GROUP)),
            dma((2, others)),
            dma((2, others)),
            *[dma((2, columns // GROUP))] * 4,
            *[dma((2,))] * 2,
            dma((rounds, 3)),
            dma((rounds, 3)),
        ],
        compiler_params=pltpu.CompilerParams(collective_id=1, has_side_effects=True, vmem_limit_bytes=VMEM_LIMIT),
    )(*operands)
    _, surface, smooth = lax.while_loop(
        lambda state: state[0] != 0, lambda state: (jnp.int32(0), *hand(whole())), (full[0], *hand((surface, smooth)))
    )
    return surface, smooth


def solution(mesh):
    placed = (
        P(None, ("groups", "surf")),
        P(("groups", "surf")),
        P(("groups", "surf")),
        P(("groups", "surf"), None),
        P(("groups", "surf"), None),
    )
    return jax.shard_map(
        body,
        mesh=mesh,
        in_specs=placed,
        out_specs=(P(None, ("groups", "surf")), P(None, ("groups", "surf"))),
        check_vma=False,
    )
```

```python
import functools

import jax
import jax.numpy as jnp
from jax import lax
from jax.experimental import pallas as pl
from jax.experimental.pallas import tpu as pltpu
from jax.sharding import PartitionSpec as P

NODES = 128
REACH = 4
SWEEPS = 4
LOW = 256
LANES = 128
PAIR = 2
BATCH = 8
BLOCK = 512
SLOTS = 256
WIDE = 2048
DEPTH = REACH * SWEEPS
MARGIN = DEPTH - REACH
GROUP = 48
PART = 8
LEVELS = 32766.0
TINY = 1e-33
VMEM_LIMIT = 60 * 1024 * 1024
smoothing = 1.5
OFFSETS = [d for d in range(-REACH, REACH + 1) if d != 0]
NOFF = len(OFFSETS)
MESH = pl.DeviceIdType.MESH


def tabulate(count, neighbours, coupling, tables):
    patches = neighbours.shape[1]
    position = lax.axis_index("surf")
    slots = lax.broadcasted_iota(jnp.int32, neighbours.shape, 1)
    distance = neighbours[...] - (position * patches + slots)
    links = coupling[...]
    along = lax.broadcasted_iota(jnp.int32, (1, patches), 1)
    alive = jnp.where(along < count[0], 1.0, 0.0).astype(jnp.float32)
    share = alive / (1.0 + smoothing * (2.0 + jnp.sum(links, axis=0, keepdims=True)))
    lines = [
        smoothing * share * jnp.sum(jnp.where(distance == offset, links, 0.0), axis=0, keepdims=True)
        for offset in OFFSETS
    ]
    lines += [share, smoothing * share, alive]
    tables[0] = jnp.zeros(tables.shape[1:], jnp.float32)
    for at, line in enumerate(lines):
        tables[0, pl.ds(at, 1), pl.ds(0, patches)] = line


def table_copy(side, tables, send_sem, recv_sem):
    position = lax.axis_index("surf")
    return pltpu.make_async_remote_copy(
        src_ref=tables.at[0],
        dst_ref=tables.at[1 + side],
        send_sem=send_sem.at[side],
        recv_sem=recv_sem.at[side],
        device_id={"surf": position + 1 if side == 0 else position - 1},
        device_id_type=MESH,
    )


def send_tables(tables, send_sem, recv_sem):
    position = lax.axis_index("surf")

    @pl.when(position < lax.axis_size("surf") - 1)
    def _():
        table_copy(0, tables, send_sem, recv_sem).start()

    @pl.when(position > 0)
    def _():
        table_copy(1, tables, send_sem, recv_sem).start()


def prepare(tables, send_sem, recv_sem, weights, fields):
    patches, columns = fields.shape[1] - 2 * DEPTH, fields.shape[2]
    position = lax.axis_index("surf")
    has_below = position > 0
    has_above = position < lax.axis_size("surf") - 1
    for side, there, landing in ((0, has_below, 0), (1, has_above, patches + DEPTH)):

        @pl.when(there)
        def _(side=side):
            table_copy(side, tables, send_sem, recv_sem).wait_recv()

        @pl.when(jnp.logical_not(there))
        def _(side=side, landing=landing):
            tables[1 + side] = jnp.zeros(tables.shape[1:], jnp.float32)
            fields[0, pl.ds(landing, DEPTH)] = jnp.zeros((DEPTH, columns, NODES), jnp.float32)

    at = lax.broadcasted_iota(jnp.int32, tables.shape[1:], 1)
    below = pltpu.roll(tables[1], (MARGIN - patches) % LANES, 1)
    own = pltpu.roll(tables[0], MARGIN, 1)
    above = pltpu.roll(tables[2], MARGIN + patches, 1)
    count = patches + 2 * MARGIN
    table = jnp.where(at < MARGIN, below, jnp.where(at < MARGIN + patches, own, jnp.where(at < count, above, 0.0)))
    turned = jnp.transpose(table)
    for at in range(NOFF + 3):
        line = jnp.broadcast_to(turned[0:count, at : at + 1], (count, LANES))
        weights[at] = jnp.broadcast_to(line[:, None, :], (count, 8, LANES))


def relaxation(acc, fields, weights, halos, surface_stage, smooth_stage, gather, aside):
    halo_out, halo_in, scale_out, scale_in, hsend_sem, hrecv_sem, ssend_sem, srecv_sem = halos
    columns = fields.shape[2]
    patches = fields.shape[1] - 2 * DEPTH
    highs = patches * NODES // LOW
    groups = columns // GROUP
    position = lax.axis_index("surf")
    has_below = position > 0
    has_above = position < lax.axis_size("surf") - 1

    def halo_copies(side, g, target):
        return [
            pltpu.make_async_remote_copy(
                src_ref=src.at[side, g],
                dst_ref=dst.at[side, g],
                send_sem=send.at[side, g],
                recv_sem=recv.at[side, g],
                device_id={"surf": target},
                device_id_type=MESH,
            )
            for src, dst, send, recv in (
                (scale_out, scale_in, ssend_sem, srecv_sem),
                (halo_out, halo_in, hsend_sem, hrecv_sem),
            )
        ]

    def put_surface(h, g):
        rows = pl.ds(g * GROUP, GROUP)
        for half in range(LOW // NODES):
            p = h * (LOW // NODES) + half
            patch = acc[pl.ds(pl.multiple_of((g * highs + h) * GROUP, 8), GROUP), pl.ds(half * NODES, NODES)]
            patch = patch * weights[NOFF + 2, MARGIN + p, 0:1, :]
            fields[0, DEPTH + p, rows] = patch
            surface_stage[rows, pl.ds(pl.multiple_of(p * NODES, NODES), NODES)] = patch

    def spread(tile):
        return jnp.concatenate([tile] * (GROUP // 8), axis=0)[None]

    def send_halo(side, g):
        @pl.when(jnp.logical_or(jnp.logical_and(side == 0, has_above), jnp.logical_and(side == 1, has_below)))
        def _():
            first = patches + side * (DEPTH - patches)
            for part in range(DEPTH // PART):
                patch = fields[0, pl.ds(first + part * PART, PART), pl.ds(g * GROUP, GROUP)]
                size = jnp.abs(patch)
                peak = functools.reduce(
                    jnp.maximum, [size[q, 8 * n : 8 * n + 8] for q in range(PART) for n in range(GROUP // 8)]
                )
                peak = jnp.maximum(peak, TINY)
                scale_out[side, g, part] = peak * (1.0 / LEVELS)
                code = jnp.floor(patch * spread(LEVELS / peak) + 0.5)
                halo_out[side, g, pl.ds(part * PART, PART)] = code.astype(jnp.int32).astype(jnp.int16)
            for copy in halo_copies(side, g, position + 1 - 2 * side):
                copy.start()

    def wait_halo(side, g):
        @pl.when(jnp.logical_or(jnp.logical_and(side == 0, has_below), jnp.logical_and(side == 1, has_above)))
        def _():
            for copy in halo_copies(side, g, position - 1 + 2 * side):
                copy.wait_recv()
            for part in range(DEPTH // PART):
                code = halo_in[side, g, pl.ds(part * PART, PART)].astype(jnp.int32).astype(jnp.float32)
                landing = side * (patches + DEPTH) + part * PART
                fields[0, pl.ds(landing, PART), pl.ds(g * GROUP, GROUP)] = code * spread(scale_in[side, g, part])

    def relax(sweep, g, first, batch):
        for low in range(g * GROUP, (g + 1) * GROUP, 8 * PAIR):
            blocks = [pl.ds(low + 8 * k, 8) for k in range(PAIR)]
            window = [[fields[sweep, first + MARGIN + q, c, :] for q in range(2 * REACH)] for c in blocks]
            for at in range(batch):
                p = first + at
                parts = [weights[line, p + MARGIN] for line in range(NOFF + 2)]
                for k, c in enumerate(blocks):
                    window[k].append(fields[sweep, p + DEPTH + REACH, c, :])
                    here = window[k][at + REACH]
                    terms = [parts[line] * window[k][at + REACH + offset] for line, offset in enumerate(OFFSETS)]
                    terms.append(parts[NOFF] * fields[0, p + DEPTH, c, :])
                    terms.append(parts[NOFF + 1] * (pltpu.roll(here, 1, 1) + pltpu.roll(here, NODES - 1, 1)))
                    while len(terms) > 1:
                        terms = [sum(terms[n : n + 2][1:], terms[n]) for n in range(0, len(terms), 2)]
                    if sweep == SWEEPS - 1:
                        smooth_stage[c, pl.ds(pl.multiple_of(p * NODES, NODES), NODES)] = terms[0]
                    else:
                        fields[sweep + 1, p + DEPTH, c, :] = terms[0]

    def relax_range(sweep, g, first, count):
        def one(step, carry):
            relax(sweep, g, first + step * BATCH, BATCH)
            return carry

        lax.fori_loop(0, count // BATCH, one, 0)

    ends = DEPTH * NODES // LOW

    for g in range(groups):
        gather(g)

        def leave(at, carry, g=g):
            side = lax.rem(position + 1 + at, 2)
            for h in range(ends):
                put_surface(h + (1 - side) * (highs - ends), g)
            send_halo(side, g)
            return carry

        lax.fori_loop(0, 2, leave, 0)
    for g in range(groups):
        for h in range(ends, highs - ends):
            put_surface(h, g)

    for g in range(groups):
        for sweep in range(SWEEPS - 1):
            edge = REACH * (sweep + 1)
            relax_range(sweep, g, edge, patches - 2 * edge)
    aside()

    def turn(at, carry):
        side = lax.rem(position + 1 + at, 2)
        for g in range(groups):
            wait_halo(side, g)
            for sweep in range(SWEEPS):
                low = REACH * sweep - MARGIN
                high = patches - REACH * (sweep + 1)
                relax(sweep, g, low + side * (high - low), DEPTH)
        return carry

    lax.fori_loop(0, 2, turn, 0)

    for side, there in ((0, has_above), (1, has_below)):

        @pl.when(there)
        def _(side=side):
            for g in range(groups):
                for copy in halo_copies(side, g, position + 1 if side == 0 else position - 1):
                    copy.wait_send()


def wait_tables(tables, send_sem, recv_sem):
    position = lax.axis_index("surf")

    @pl.when(position < lax.axis_size("surf") - 1)
    def _():
        table_copy(0, tables, send_sem, recv_sem).wait_send()

    @pl.when(position > 0)
    def _():
        table_copy(1, tables, send_sem, recv_sem).wait_send()


def kernel(
    chunk,
    sens,
    owner,
    count,
    neighbours_in,
    coupling_in,
    surface_stage,
    smooth_stage,
    neighbours,
    coupling,
    link_sem,
    values,
    owners,
    masked,
    low_hot,
    acc,
    fields,
    weights,
    tables,
    halo_out,
    halo_in,
    scale_out,
    scale_in,
    out_sem,
    load_sem,
    oload_sem,
    send_sem,
    recv_sem,
    osend_sem,
    orecv_sem,
    hsend_sem,
    hrecv_sem,
    ssend_sem,
    srecv_sem,
    tsend_sem,
    trecv_sem,
):
    columns, faces = sens.shape
    patches = neighbours.shape[1]
    span = patches * NODES
    highs = span // LOW
    chunks = faces // chunk
    pieces = chunk // LANES
    orow = faces // LANES
    position = lax.axis_index("surf")
    peers = lax.axis_size("surf")
    has_below = position > 0
    has_above = position < peers - 1

    def local_load(k):
        return pltpu.make_async_copy(sens.at[:, pl.ds(k * chunk, chunk)], values.at[0, k], load_sem.at[k])

    def face_copy(side, k):
        target = position + 1 if side == 0 else position - 1
        return pltpu.make_async_remote_copy(
            src_ref=sens.at[:, pl.ds(k * chunk, chunk)],
            dst_ref=values.at[1 + side, k],
            send_sem=send_sem.at[side, k],
            recv_sem=recv_sem.at[side, k],
            device_id={"surf": target},
            device_id_type=MESH,
        )

    def owner_copy(side):
        target = position + 1 if side == 0 else position - 1
        return pltpu.make_async_remote_copy(
            src_ref=owner,
            dst_ref=owners.at[1 + side],
            send_sem=osend_sem.at[side],
            recv_sem=orecv_sem.at[side],
            device_id={"surf": target},
            device_id_type=MESH,
        )

    own_owner = pltpu.make_async_copy(owner, owners.at[0], oload_sem)
    own_owner.start()
    link_copies = (
        pltpu.make_async_copy(neighbours_in, neighbours, link_sem.at[0]),
        pltpu.make_async_copy(coupling_in, coupling, link_sem.at[1]),
    )
    for link_copy in link_copies:
        link_copy.start()
    for k in range(chunks):
        local_load(k).start()

    barrier = pltpu.get_barrier_semaphore()

    @pl.when(has_below)
    def _():
        pl.semaphore_signal(barrier, inc=1, device_id={"surf": position - 1}, device_id_type=MESH)

    @pl.when(has_above)
    def _():
        pl.semaphore_signal(barrier, inc=1, device_id={"surf": position + 1}, device_id_type=MESH)

    both = jnp.logical_and(has_below, has_above)

    @pl.when(both)
    def _():
        pl.semaphore_wait(barrier, 2)

    @pl.when(jnp.logical_not(both))
    def _():
        pl.semaphore_wait(barrier, 1)

    @pl.when(has_above)
    def _():
        owner_copy(0).start()

    @pl.when(has_below)
    def _():
        owner_copy(1).start()

    for k in range(chunks):

        @pl.when(has_above)
        def _(k=k):
            face_copy(0, k).start()

        @pl.when(has_below)
        def _(k=k):
            face_copy(1, k).start()

    for link_copy in link_copies:
        link_copy.wait()
    tabulate(count, neighbours, coupling, tables)
    send_tables(tables, tsend_sem, trecv_sem)
    prepare(tables, tsend_sem, trecv_sem, weights, fields)

    acc[...] = jnp.zeros_like(acc)
    first_node = position * span
    low_rows = lax.broadcasted_iota(jnp.int32, (LOW, LANES), 0)

    def add_chunk(slot, k):
        for j in range(pieces):
            local = owners[slot, pl.ds(k * pieces + j, 1), :] - first_node
            high = (local >> 8).astype(jnp.float32).astype(jnp.bfloat16)
            low = local & (LOW - 1)
            lanes = pl.ds(j * LANES, LANES)
            low_hot[:, lanes] = jnp.where(low_rows == low, 1.0, 0.0).astype(jnp.bfloat16)
            vals = values[slot, k, :, lanes]
            high_full = jnp.broadcast_to(high, vals.shape)
            for h in range(highs):
                kept = jnp.where(high_full == jnp.bfloat16(h), vals, jnp.bfloat16(0))
                for g in range(columns // GROUP):
                    masked[pl.ds((g * highs + h) * GROUP, GROUP), lanes] = kept[g * GROUP : (g + 1) * GROUP]
        acc[...] += lax.dot_general(
            masked[...],
            low_hot[...],
            (((1,), (1,)), ((), ())),
            preferred_element_type=jnp.float32,
        )

    own_owner.wait()

    def step(s, carry):
        is_own = s < chunks
        t = jnp.maximum(s - chunks, 0)
        side = lax.rem(t, 2)
        k = jnp.where(is_own, s, t // 2)
        slot = jnp.where(is_own, 0, 1 + side)

        @pl.when(is_own)
        def _():
            local_load(k).wait()

        from_below = jnp.logical_and(jnp.logical_not(is_own), side == 0)
        from_above = jnp.logical_and(jnp.logical_not(is_own), side == 1)

        @pl.when(jnp.logical_and(from_below, has_below))
        def _():
            @pl.when(t == 0)
            def _():
                owner_copy(0).wait_recv()

            face_copy(0, k).wait_recv()

        @pl.when(jnp.logical_and(from_above, has_above))
        def _():
            @pl.when(t == 1)
            def _():
                owner_copy(1).wait_recv()

            face_copy(1, k).wait_recv()

        present = jnp.logical_or(
            is_own,
            jnp.logical_or(jnp.logical_and(side == 0, has_below), jnp.logical_and(side == 1, has_above)),
        )

        @pl.when(present)
        def _():
            add_chunk(slot, k)

        return carry

    lax.fori_loop(0, 3 * chunks, step, 0)

    halos = (halo_out, halo_in, scale_out, scale_in, hsend_sem, hrecv_sem, ssend_sem, srecv_sem)
    relaxation(acc, fields, weights, halos, surface_stage, smooth_stage, lambda g: None, lambda: None)
    wait_tables(tables, tsend_sem, trecv_sem)

    for side, there in ((0, has_above), (1, has_below)):

        @pl.when(there)
        def _(side=side):
            owner_copy(side).wait_send()
            for k in range(chunks):
                face_copy(side, k).wait_send()


def flag_masks(peers):
    bits = peers.bit_length() - 1
    return [[mask << at for mask in ((1, 2, 3) if at + 1 < bits else (1,))] for at in range(0, bits, 2)]


def packed_kernel(
    sens,
    owner,
    count,
    neighbours_in,
    coupling_in,
    surface_stage,
    smooth_stage,
    full_out,
    neighbours,
    coupling,
    link_sem,
    values,
    owners,
    nodes,
    spots,
    values_out,
    nodes_out,
    sort_hot,
    masked,
    low_hot,
    acc,
    fields,
    weights,
    tables,
    halo_out,
    halo_in,
    scale_out,
    scale_in,
    flags,
    flags_in,
    load_sem,
    oload_sem,
    send_sem,
    recv_sem,
    nsend_sem,
    nrecv_sem,
    hsend_sem,
    hrecv_sem,
    ssend_sem,
    srecv_sem,
    tsend_sem,
    trecv_sem,
    fsend_sem,
    frecv_sem,
):
    columns, faces = sens.shape
    patches = neighbours.shape[1]
    span = patches * NODES
    highs = span // LOW
    rows = faces // LANES
    owns = faces // WIDE
    blocks = faces // BLOCK
    pieces = WIDE // LANES
    fit = WIDE // SLOTS
    others = blocks // fit
    groups = columns // GROUP
    position = lax.axis_index("surf")
    peers = lax.axis_size("surf")
    masks = flag_masks(peers)
    has_below = position > 0
    has_above = position < peers - 1
    first_node = position * span

    def partner(mask):
        other = position
        for bit in range(peers.bit_length()):
            size = 2**bit
            if mask & size:
                other = other + size - 2 * size * (lax.div(position, size) % 2)
        return other

    def local_load(k):
        return pltpu.make_async_copy(sens.at[:, pl.ds(k * WIDE, WIDE)], values.at[k], load_sem.at[k])

    def value_copy(side, k, q, g):
        target = position + 1 if side == 0 else position - 1
        lanes = pl.ds(pl.multiple_of(q * SLOTS, SLOTS), SLOTS)
        return pltpu.make_async_remote_copy(
            src_ref=values_out.at[side, k, pl.ds(g * GROUP, GROUP), lanes],
            dst_ref=values.at[owns + 2 * k + side, pl.ds(g * GROUP, GROUP), lanes],
            send_sem=send_sem.at[side, k, q, g],
            recv_sem=recv_sem.at[side, k, q, g],
            device_id={"surf": target},
            device_id_type=MESH,
        )

    def node_copy(side, k):
        target = position + 1 if side == 0 else position - 1
        return pltpu.make_async_remote_copy(
            src_ref=nodes_out.at[side, k],
            dst_ref=nodes.at[owns + 2 * k + side],
            send_sem=nsend_sem.at[side, k],
            recv_sem=nrecv_sem.at[side, k],
            device_id={"surf": target},
            device_id_type=MESH,
        )

    def flag_copies(step):
        return [
            pltpu.make_async_remote_copy(
                src_ref=flags.at[step],
                dst_ref=flags_in.at[step, n],
                send_sem=fsend_sem.at[step, n],
                recv_sem=frecv_sem.at[step, n],
                device_id={"surf": partner(mask)},
                device_id_type=MESH,
            )
            for n, mask in enumerate(masks[step])
        ]

    own_owner = pltpu.make_async_copy(owner, owners, oload_sem)
    own_owner.start()
    for k in range(owns):
        local_load(k).start()
    link_copies = (
        pltpu.make_async_copy(neighbours_in, neighbours, link_sem.at[0]),
        pltpu.make_async_copy(coupling_in, coupling, link_sem.at[1]),
    )
    for link_copy in link_copies:
        link_copy.start()

    barrier = pltpu.get_barrier_semaphore()

    @pl.when(has_below)
    def _():
        pl.semaphore_signal(barrier, inc=1, device_id={"surf": position - 1}, device_id_type=MESH)

    @pl.when(has_above)
    def _():
        pl.semaphore_signal(barrier, inc=1, device_id={"surf": position + 1}, device_id_type=MESH)

    greeted = [mask for step in masks for mask in step]
    for mask in greeted:
        pl.semaphore_signal(barrier, inc=1, device_id={"surf": partner(mask)}, device_id_type=MESH)

    own_owner.wait()
    local = owners[...] - first_node
    for k in range(owns):
        nodes[k] = local[k * pieces : (k + 1) * pieces]
    leaves = jnp.concatenate([local - (span - 1), -local], axis=0) > 0
    marks = jnp.where(leaves, 1.0, 0.0).astype(jnp.bfloat16)
    down = lax.broadcasted_iota(jnp.int32, (LANES, LANES), 0)
    along = lax.broadcasted_iota(jnp.int32, (LANES, LANES), 1)
    earlier = jnp.where(down < along, 1.0, 0.0).astype(jnp.bfloat16)
    block_rows = BLOCK // LANES
    down = lax.broadcasted_iota(jnp.int32, (2 * rows, 2 * rows), 0)
    along = lax.broadcasted_iota(jnp.int32, (2 * rows, 2 * rows), 1)
    same = lax.div(down, block_rows) == lax.div(along, block_rows)
    above = jnp.where(same & (along < down), 1.0, 0.0).astype(jnp.bfloat16)
    sums = jnp.dot(marks, jnp.ones((LANES, LANES), jnp.bfloat16), preferred_element_type=jnp.float32)
    place = jnp.dot(marks, earlier, preferred_element_type=jnp.float32)
    place += jnp.dot(above, sums.astype(jnp.bfloat16), preferred_element_type=jnp.float32)
    spots[...] = jnp.where(leaves, place, 2.0 * SLOTS)
    over = jnp.where(leaves & (place > SLOTS - 0.5), 1.0, 0.0)
    flags[0] = functools.reduce(jnp.maximum, [over[8 * n : 8 * n + 8] for n in range(2 * rows // 8)])

    for link_copy in link_copies:
        link_copy.wait()
    tabulate(count, neighbours, coupling, tables)
    both = jnp.logical_and(has_below, has_above)

    @pl.when(both)
    def _():
        pl.semaphore_wait(barrier, 2 + len(greeted))

    @pl.when(jnp.logical_not(both))
    def _():
        pl.semaphore_wait(barrier, 1 + len(greeted))

    for copy in flag_copies(0):
        copy.start()
    send_tables(tables, tsend_sem, trecv_sem)
    for k in range(owns):
        local_load(k).wait()

    slot_rows = lax.broadcasted_iota(jnp.int32, (SLOTS, LANES), 0).astype(jnp.float32).astype(jnp.bfloat16)
    code_rows = lax.broadcasted_iota(jnp.int32, (16, LANES), 0)
    in_wide = WIDE // BLOCK

    def pack(k, carry):
        for q in range(fit):
            at = k * fit + q
            codes = []
            for j in range(block_rows):
                lanes = pl.ds(j * LANES, LANES)
                row = at * block_rows + j
                node = owners[pl.ds(row, 1), :]
                high = jnp.broadcast_to((node >> 8) & (highs - 1), (16, LANES))
                low = jnp.broadcast_to(node & (LOW - 1), (16, LANES))
                code = jnp.where(code_rows == 0, high, jnp.where(code_rows == 1, low, 0))
                codes.append(code.astype(jnp.float32).astype(jnp.bfloat16))
                for side in range(2):
                    spot = spots[pl.ds(side * rows + row, 1), :].astype(jnp.bfloat16)
                    spot = jnp.broadcast_to(spot, (SLOTS, LANES))
                    sort_hot[q % 2, pl.ds(side * SLOTS, SLOTS), lanes] = jnp.where(
                        spot == slot_rows, jnp.bfloat16(1), jnp.bfloat16(0)
                    )
            own = values[k * (fit // in_wide) + q // in_wide, :, pl.ds((q % in_wide) * BLOCK, BLOCK)]
            left = jnp.concatenate([own, jnp.concatenate(codes, axis=1)], axis=0)
            moved = lax.dot_general(
                left, sort_hot[q % 2], (((1,), (1,)), ((), ())), preferred_element_type=jnp.float32
            )
            node = (moved[columns : columns + 1] * LOW + moved[columns + 1 : columns + 2]).astype(jnp.int32)
            for side, there in ((0, has_above), (1, has_below)):
                values_out[side, k, :, pl.ds(q * SLOTS, SLOTS)] = moved[
                    0:columns, side * SLOTS : (side + 1) * SLOTS
                ].astype(jnp.bfloat16)
                for j in range(SLOTS // LANES):
                    nodes_out[side, k, pl.ds(q * (SLOTS // LANES) + j, 1), :] = node[
                        :, side * SLOTS + j * LANES : side * SLOTS + (j + 1) * LANES
                    ]

                @pl.when(there)
                def _(side=side, q=q):
                    value_copy(side, k, q, 0).start()

        for side, there in ((0, has_above), (1, has_below)):

            @pl.when(there)
            def _(side=side):
                node_copy(side, k).start()

        return carry

    lax.fori_loop(0, others, pack, 0)

    def send_more(k, carry):
        for side, there in ((0, has_above), (1, has_below)):

            @pl.when(there)
            def _(side=side):
                for g in range(1, groups):
                    for q in range(fit):
                        value_copy(side, k, q, g).start()

        return carry

    lax.fori_loop(0, others, send_more, 0)

    acc[...] = jnp.zeros_like(acc)

    def add_chunk(s, g):
        for j in range(pieces):
            node = nodes[s, pl.ds(j, 1), :]
            high = (node >> 8).astype(jnp.float32).astype(jnp.bfloat16)
            low = (node & (LOW - 1)).astype(jnp.float32).astype(jnp.bfloat16)
            lanes = pl.ds(j * LANES, LANES)
            low_hot[:, lanes] = jnp.where(
                slot_rows == jnp.broadcast_to(low, (LOW, LANES)), jnp.bfloat16(1), jnp.bfloat16(0)
            )
            vals = values[s, pl.ds(g * GROUP, GROUP), lanes]
            high_full = jnp.broadcast_to(high, vals.shape)
            for h in range(highs):
                masked[pl.ds(h * GROUP, GROUP), lanes] = jnp.where(
                    high_full == jnp.bfloat16(h), vals, jnp.bfloat16(0)
                )
        acc[pl.ds(g * highs * GROUP, highs * GROUP)] += lax.dot_general(
            masked[...], low_hot[...], (((1,), (1,)), ((), ())), preferred_element_type=jnp.float32
        )

    def pass_flags(step):
        total = flags[step]
        for n, copy in enumerate(flag_copies(step)):
            copy.wait_recv()
            total = jnp.maximum(total, flags_in[step, n])
        flags[step + 1] = total
        if step + 1 < len(masks):
            for copy in flag_copies(step + 1):
                copy.start()

    def aside():
        for step in range(1, len(masks) - 1):
            pass_flags(step)

    def step(g, s, carry):
        t = jnp.maximum(s - owns, 0)
        side = lax.rem(position + 1 + lax.div(t, others), 2)
        k = lax.rem(t, others)
        is_own = s < owns
        slot = jnp.where(is_own, s, owns + 2 * k + side)
        from_below = jnp.logical_and(jnp.logical_not(is_own), jnp.logical_and(side == 0, has_below))
        from_above = jnp.logical_and(jnp.logical_not(is_own), jnp.logical_and(side == 1, has_above))

        if g == 0:

            @pl.when(s == owns)
            def _():
                if len(masks) > 1:
                    pass_flags(0)
                prepare(tables, tsend_sem, trecv_sem, weights, fields)

        @pl.when(from_below)
        def _():
            if g == 0:
                node_copy(0, k).wait_recv()
            for q in range(fit):
                value_copy(0, k, q, g).wait_recv()

        @pl.when(from_above)
        def _():
            if g == 0:
                node_copy(1, k).wait_recv()
            for q in range(fit):
                value_copy(1, k, q, g).wait_recv()

        @pl.when(jnp.logical_or(is_own, jnp.logical_or(from_below, from_above)))
        def _():
            add_chunk(slot, g)

        return carry

    def gather(g):
        lax.fori_loop(0, owns + 2 * others, functools.partial(step, g), 0)

    halos = (halo_out, halo_in, scale_out, scale_in, hsend_sem, hrecv_sem, ssend_sem, srecv_sem)
    relaxation(acc, fields, weights, halos, surface_stage, smooth_stage, gather, aside)
    wait_tables(tables, tsend_sem, trecv_sem)
    pass_flags(len(masks) - 1)
    full_out[0] = jnp.max(flags[len(masks)]).astype(jnp.int32)

    for step in range(len(masks)):
        for copy in flag_copies(step):
            copy.wait_send()
    for side, there in ((0, has_above), (1, has_below)):

        @pl.when(there)
        def _(side=side):
            for k in range(others):
                node_copy(side, k).wait_send()
                for q in range(fit):
                    for g in range(groups):
                        value_copy(side, k, q, g).wait_send()


def hand_over(surface, smooth, surface_out, smooth_out, out_sem):
    copies = [
        pltpu.make_async_copy(surface, surface_out, out_sem.at[0]),
        pltpu.make_async_copy(smooth, smooth_out, out_sem.at[1]),
    ]
    for copy in copies:
        copy.start()
    for copy in copies:
        copy.wait()


def body(sensitivity, owner, patch_count, neighbours, coupling):
    columns, faces = sensitivity.shape
    patches = neighbours.shape[0]
    span = patches * NODES
    rows = faces // LANES
    chunk = min(512, faces)
    chunks = faces // chunk
    highs = span // LOW
    hbm = pl.BlockSpec(memory_space=pltpu.HBM)
    vmem = pl.BlockSpec(memory_space=pltpu.VMEM)
    smem = pl.BlockSpec(memory_space=pltpu.SMEM)
    links = neighbours.T.shape
    out = jax.ShapeDtypeStruct((columns, span), jnp.float32)
    kept = pltpu.VMEM((columns, span), jnp.float32)
    dma = pltpu.SemaphoreType.DMA
    operands = (sensitivity, owner.reshape(rows, LANES), patch_count, neighbours.T, coupling.T)
    peers = lax.axis_size("surf")
    link_scratch = [pltpu.VMEM(links, jnp.int32), pltpu.VMEM(links, jnp.float32), dma((2,))]
    field_scratch = [
        pltpu.VMEM((highs * columns, LOW), jnp.float32),
        pltpu.VMEM((SWEEPS, patches + 2 * DEPTH, columns, NODES), jnp.float32),
        pltpu.VMEM((NOFF + 3, patches + 2 * MARGIN, 8, LANES), jnp.float32),
        pltpu.VMEM((3, 16, LANES), jnp.float32),
        *[pltpu.VMEM((2, columns // GROUP, DEPTH, GROUP, NODES), jnp.int16)] * 2,
        *[pltpu.VMEM((2, columns // GROUP, DEPTH // PART, 8, NODES), jnp.float32)] * 2,
    ]

    def hand(outputs):
        return pl.pallas_call(
            hand_over,
            out_shape=(out, out),
            in_specs=[vmem, vmem],
            out_specs=(hbm, hbm),
            scratch_shapes=[dma((2,))],
            compiler_params=pltpu.CompilerParams(vmem_limit_bytes=16 * 1024 * 1024),
        )(*outputs)

    def whole():
        return pl.pallas_call(
            functools.partial(kernel, chunk),
            out_shape=(kept, kept),
            in_specs=[hbm, hbm, smem, hbm, hbm],
            out_specs=(vmem, vmem),
            scratch_shapes=[
                *link_scratch,
                pltpu.VMEM((3, chunks, columns, chunk), jnp.bfloat16),
                pltpu.VMEM((3, rows, LANES), jnp.int32),
                pltpu.VMEM((highs * columns, chunk), jnp.bfloat16),
                pltpu.VMEM((LOW, chunk), jnp.bfloat16),
                *field_scratch,
                dma((2,)),
                dma((chunks,)),
                dma,
                dma((2, chunks)),
                dma((2, chunks)),
                dma((2,)),
                dma((2,)),
                *[dma((2, columns // GROUP))] * 4,
            *[dma((2,))] * 2,
            ],
            compiler_params=pltpu.CompilerParams(
                collective_id=0, has_side_effects=True, vmem_limit_bytes=VMEM_LIMIT
            ),
        )(*operands)

    if faces % WIDE or highs & (highs - 1) or peers & (peers - 1) or peers < 2:
        return hand(whole())

    owns, blocks, fit, rounds = faces // WIDE, faces // BLOCK, WIDE // SLOTS, len(flag_masks(peers))
    others = blocks // fit
    surface, smooth, full = pl.pallas_call(
        packed_kernel,
        out_shape=(kept, kept, jax.ShapeDtypeStruct((1,), jnp.int32)),
        in_specs=[hbm, hbm, smem, hbm, hbm],
        out_specs=(vmem, vmem, smem),
        scratch_shapes=[
            *link_scratch,
            pltpu.VMEM((owns + 2 * others, columns, WIDE), jnp.bfloat16),
            pltpu.VMEM((rows, LANES), jnp.int32),
            pltpu.VMEM((owns + 2 * others, WIDE // LANES, LANES), jnp.int32),
            pltpu.VMEM((2 * rows, LANES), jnp.float32),
            pltpu.VMEM((2, others, columns, WIDE), jnp.bfloat16),
            pltpu.VMEM((2, others, WIDE // LANES, LANES), jnp.int32),
            pltpu.VMEM((2, 2 * SLOTS, BLOCK), jnp.bfloat16),
            pltpu.VMEM((highs * GROUP, WIDE), jnp.bfloat16),
            pltpu.VMEM((LOW, WIDE), jnp.bfloat16),
            *field_scratch,
            pltpu.VMEM((rounds + 1, 8, LANES), jnp.float32),
            pltpu.VMEM((rounds, 3, 8, LANES), jnp.float32),
            dma((owns,)),
            dma,
            dma((2, others, fit, columns // GROUP)),
            dma((2, others, fit, columns // GROUP)),
            dma((2, others)),
            dma((2, others)),
            *[dma((2, columns // GROUP))] * 4,
            *[dma((2,))] * 2,
            dma((rounds, 3)),
            dma((rounds, 3)),
        ],
        compiler_params=pltpu.CompilerParams(collective_id=1, has_side_effects=True, vmem_limit_bytes=VMEM_LIMIT),
    )(*operands)
    _, surface, smooth = lax.while_loop(
        lambda state: state[0] != 0, lambda state: (jnp.int32(0), *hand(whole())), (full[0], *hand((surface, smooth)))
    )
    return surface, smooth


def solution(mesh):
    placed = (
        P(None, ("groups", "surf")),
        P(("groups", "surf")),
        P(("groups", "surf")),
        P(("groups", "surf"), None),
        P(("groups", "surf"), None),
    )
    return jax.shard_map(
        body,
        mesh=mesh,
        in_specs=placed,
        out_specs=(P(None, ("groups", "surf")), P(None, ("groups", "surf"))),
        check_vma=False,
    )
```
